256 devices in a mesh: lat: 16 (over y_lo, x, core), lon: 16 (over z, y_hi).
Axes of the slice: x: 4, y: 4 (y_hi: 2, y_lo: 2; y = y_hi * 2 + y_lo), z: 8, core: 2. Of those that a mesh axis runs over, the one named last changes fastest.
Arguments:
- tokens: bfloat16 [256, 256, 1024], P('lat', 'lon'), may hold values from -36 to 36
- gain_attn: float32 [1024], replicated, may hold values from 0.5 to 1.5
- w_qkv: bfloat16 [1024, 1536], replicated, may hold values from -0.1875 to 0.1875
- logit_scale: float32 [8], replicated, may hold values from 4 to 20
- w_out: bfloat16 [512, 1024], replicated, may hold values from -0.5 to 0.5
- gain_ffn: float32 [1024], replicated, may hold values from 0.5 to 1.5
- w_up: bfloat16 [1024, 2048], replicated, may hold values from -0.1875 to 0.1875
- conv_taps: float32 [3, 3, 2048], replicated, may hold values from -2 to 2
Outputs:
- ffn_hidden: bfloat16 [256, 256, 2048], P('lat', 'lon')
The draws below stay inside these ranges and needn't reach their ends.
All inputs are finite; a program needn't handle non-finite values.
Results may differ from the reference program's by a relative error of at most 0.008.
Values may be sent and summed in bfloat16 or wider, within the bound.
A program may use at most 64 MiB of HBM per device.

```python
import math
import jax
import jax.numpy as jnp
from jax import lax

D = 1024
HEADS = 8
HEAD_DIM = 64
HID = 2048
RADIUS = 6
INNER = 512
GRID_LAT = 256
GRID_LON = 256


def draw_tokens(key, part):
    key = jax.random.fold_in(key, 7)
    primary_key, column_key, row_key = jax.random.split(key, 3)
    extent = (GRID_LAT, GRID_LON, D)
    primary = jax.random.normal(primary_key, extent, jnp.float32)
    primary = jnp.clip(primary, -6.0, 6.0)
    column_scale = jnp.exp(jax.random.uniform(column_key, (D,), jnp.float32, math.log(0.3), math.log(3.0)))
    row_scale = jnp.exp(jax.random.uniform(row_key, (GRID_LAT, GRID_LON, 1), jnp.float32, math.log(0.5), math.log(2.0)))
    return (primary * column_scale * row_scale).astype(jnp.bfloat16)


def scatter_about(rng, shape, width, reach, held_as=jnp.bfloat16):
    drawn = width * jax.random.normal(rng, shape, jnp.float32)
    return jnp.clip(drawn, min=-reach, max=reach).astype(held_as)


def setup_inputs(seed: int = 0) -> dict:
    seeds = jax.random.split(jax.random.key(seed), 9)
    tokens = draw_tokens(jax.random.fold_in(seeds[8], 71), 0)
    gain_attn = jnp.clip(1.0 + 0.1 * jax.random.normal(seeds[1], (D,), jnp.float32), 0.5, 1.5)
    w_qkv = scatter_about(seeds[2], (D, 3 * INNER), D ** -0.5, 0.1875)
    logit_scale = jnp.clip(jnp.exp(jax.random.uniform(seeds[3], (HEADS,), jnp.float32, math.log(4.0), math.log(20.0))), 4.0, 20.0)
    w_out = scatter_about(seeds[4], (INNER, D), (INNER // 4) ** -0.5, 0.5)
    gain_ffn = jnp.clip(1.0 + 0.1 * jax.random.normal(seeds[5], (D,), jnp.float32), 0.5, 1.5)
    w_up = scatter_about(seeds[6], (D, HID), D ** -0.5, 0.1875)
    conv_taps = scatter_about(seeds[7], (3, 3, HID), 9 ** -0.5, 2.0, jnp.float32)
    return dict(tokens=tokens, gain_attn=gain_attn, w_qkv=w_qkv, logit_scale=logit_scale, w_out=w_out, gain_ffn=gain_ffn, w_up=w_up, conv_taps=conv_taps)


def layer_norm(values_in, gain):
    widened = values_in.astype(jnp.float32)
    centre = lax.optimization_barrier(jnp.mean(widened, -1, keepdims=True))
    spread = lax.optimization_barrier(jnp.mean((widened - centre) ** 2, -1, keepdims=True))
    return (widened - centre) * lax.rsqrt(spread + 1e-05) * gain

def heads_norm(vectors, factor):
    return vectors * lax.rsqrt(lax.optimization_barrier(jnp.sum(vectors * vectors, -1, keepdims=True)) + 1e-06) * factor

def wrap_pad(field, margin):
    padded = jnp.pad(field, [(margin, margin)] + [(0, 0)] * (field.ndim - 1))
    return jnp.concatenate([padded[:, -margin:], padded, padded[:, :margin]], 1)

def reference(tokens, gain_attn, w_qkv, logit_scale, w_out, gain_ffn, w_up, conv_taps):
    height, breadth = (tokens.shape[0], tokens.shape[1])
    normed = layer_norm(tokens, gain_attn).astype(jnp.bfloat16).reshape(-1, D)
    projected = jnp.dot(normed, w_qkv, preferred_element_type=jnp.float32)
    queries = heads_norm(projected[:, :INNER].reshape(height, breadth, HEADS, HEAD_DIM), logit_scale[:, None]).astype(jnp.bfloat16)
    key_heads = heads_norm(projected[:, INNER:2 * INNER].reshape(height, breadth, HEADS, HEAD_DIM), 1.0).astype(jnp.bfloat16)
    values = projected[:, 2 * INNER:].reshape(height, breadth, HEADS, HEAD_DIM).astype(jnp.bfloat16)
    key_pad = wrap_pad(key_heads, RADIUS)
    value_pad = wrap_pad(values, RADIUS)
    row_valid = jnp.pad(jnp.ones((height,), bool), RADIUS)
    span = 2 * RADIUS + 1
    query_wide = queries.astype(jnp.float32)

    def accumulate(carry, offset):
        numerator, denominator = carry
        row_shift = (offset // span).astype(jnp.int32)
        col_shift = (offset % span).astype(jnp.int32)
        shifted_keys = lax.dynamic_slice_in_dim(lax.dynamic_slice_in_dim(key_pad, row_shift, height, 0), col_shift, breadth, 1)
        shifted_values = lax.dynamic_slice_in_dim(lax.dynamic_slice_in_dim(value_pad, row_shift, height, 0), col_shift, breadth, 1)
        inside = lax.dynamic_slice_in_dim(row_valid, row_shift, height, 0)
        scores = lax.optimization_barrier(jnp.sum(query_wide * shifted_keys.astype(jnp.float32), -1))
        weights = jnp.where(inside[:, None, None], jnp.exp(scores), 0.0)
        rounded = lax.optimization_barrier(weights.astype(jnp.bfloat16))
        numerator = numerator + rounded.astype(jnp.float32)[..., None] * shifted_values.astype(jnp.float32)
        return ((numerator, denominator + weights), None)
    start = (jnp.zeros((height, breadth, HEADS, HEAD_DIM), jnp.float32), jnp.zeros((height, breadth, HEADS), jnp.float32))
    (numerator, denominator), _ = lax.scan(accumulate, start, jnp.arange(span * span, dtype=jnp.int32))
    attended = (numerator / denominator[..., None]).astype(jnp.bfloat16).reshape(-1, INNER)
    stream = tokens.astype(jnp.float32).reshape(-1, D) + jnp.dot(attended, w_out, preferred_element_type=jnp.float32)
    normed_ffn = layer_norm(stream, gain_ffn).astype(jnp.bfloat16)
    hidden = jnp.dot(normed_ffn, w_up, preferred_element_type=jnp.float32).astype(jnp.bfloat16).reshape(height, breadth, HID)
    padded = wrap_pad(hidden, 1)
    filtered = jnp.zeros((height, breadth, HID), jnp.float32)
    for row_tap in range(3):
        for col_tap in range(3):
            filtered = filtered + padded[row_tap:row_tap + height, col_tap:col_tap + breadth].astype(jnp.float32) * conv_taps[row_tap, col_tap]
    return jax.nn.gelu(filtered, approximate=False).astype(jnp.bfloat16)
```

```python
import functools

import jax
import jax.numpy as jnp
from jax import lax
from jax.experimental import pallas as pl
from jax.experimental.pallas import tpu as pltpu
from jax.sharding import PartitionSpec as P

D = 1024
HEADS = 8
HEAD_DIM = 64
HID = 2048
RADIUS = 6
INNER = 512

SIDE = 16
REACH = RADIUS + 1
ROWS = SIDE + 2 * REACH
RING = SIDE + 2
HALF = RING * 8
EDGE = 32
STRIP = SIDE * REACH
CORNER = 64
CUT = STRIP - CORNER
KEYS_C = 512
KEYS_S = 256
PAIRS = HEADS // 2
TILE = 256
BF = jnp.bfloat16
F32 = jnp.float32
MESH = pl.DeviceIdType.MESH
FAR = -1e30

DOWN, UP, W_LOW, W_HIGH, E_LOW, E_HIGH, W_DOWN, W_UP, E_DOWN, E_UP = range(10)
L_TOK, L_GA, L_GF, L_TAPS, L_WK, L_WV, L_WQ, L_WO, L_WU = range(9)


def iota(shape, dim):
    return lax.broadcasted_iota(jnp.int32, shape, dim)


def div7(n):
    return (n * 9363) >> 16


def norm_rows(x, gain):
    centre = jnp.mean(x, -1, keepdims=True)
    moved = x - centre
    spread = jnp.mean(moved * moved, -1, keepdims=True)
    return moved * lax.rsqrt(spread + 1e-05) * gain


def gelu(x):
    size = jnp.abs(x)
    t = 1.0 / (1.0 + size * (0.3275911 * 0.7071067811865476))
    poly = 0.5 * 1.061405429
    for c in (-1.453152027, 1.421413741, -0.284496736, 0.254829592):
        poly = poly * t + 0.5 * c
    tail = poly * t * jnp.exp(x * x * -0.5)
    return jnp.maximum(x, 0.0) - size * tail


def kernel(
    tok, ga_h, wqkv_h, scale, wo_h, gf_h, wu_h, taps_h, out,
    ct, wt, et, xn, send_e, send_w, wk, wv, wq, wo, wu, ga, gf, taps,
    kc, vc, kw, vw, qc, qe, xres, acc_n, acc_d, bias_c, bias_s, bias_e,
    nf, hid_l, hid_r, ob, lsem, osem, ss, rs,
):
    lat, lon = lax.axis_index("lat"), lax.axis_index("lon")
    n_lat, n_lon = lax.axis_size("lat"), lax.axis_size("lon")
    east, west = lax.rem(lon + 1, n_lon), lax.rem(lon + n_lon - 1, n_lon)
    north_ok, south_ok = lat > 0, lat < n_lat - 1

    loc = [
        pltpu.make_async_copy(s, d, lsem.at[i])
        for i, (s, d) in enumerate((
            (tok, ct.at[pl.ds(REACH, SIDE)]),
            (ga_h, ga), (gf_h, gf), (taps_h, taps),
            (wqkv_h.at[:, pl.ds(INNER, INNER)], wk),
            (wqkv_h.at[:, pl.ds(2 * INNER, INNER)], wv),
            (wqkv_h.at[:, pl.ds(0, INNER)], wq),
            (wo_h, wo), (wu_h, wu),
        ))
    ]
    for c in loc:
        c.start()

    def remote(i, src, dst, device):
        return pltpu.make_async_remote_copy(
            src_ref=src, dst_ref=dst, send_sem=ss.at[i], recv_sem=rs.at[i],
            device_id=device, device_id_type=MESH,
        )

    below, above = (lat + 1, lon), (lat - 1, lon)
    to_e, to_w = (lat, east), (lat, west)
    low, high = pl.ds(CUT, CORNER), pl.ds(0, CUT)
    low_d, high_d = pl.ds(CORNER + CUT, CORNER), pl.ds(CORNER, CUT)
    top_d, bot_d = pl.ds(0, CORNER), pl.ds(CORNER + STRIP, CORNER)
    first_d = pl.ds(CORNER, CORNER)
    rem = [
        remote(DOWN, tok.at[pl.ds(SIDE - REACH, REACH)], ct.at[pl.ds(0, REACH)], below),
        remote(UP, tok.at[pl.ds(0, REACH)], ct.at[pl.ds(REACH + SIDE, REACH)], above),
        remote(W_LOW, send_e.at[low], wt.at[low_d], to_e),
        remote(W_HIGH, send_e.at[high], wt.at[high_d], to_e),
        remote(E_LOW, send_w.at[low], et.at[low_d], to_w),
        remote(E_HIGH, send_w.at[high], et.at[high_d], to_w),
        remote(W_DOWN, wt.at[low_d], wt.at[top_d], below),
        remote(W_UP, wt.at[first_d], wt.at[bot_d], above),
        remote(E_DOWN, et.at[low_d], et.at[top_d], below),
        remote(E_UP, et.at[first_d], et.at[bot_d], above),
    ]
    goes_south, goes_north = (DOWN, W_DOWN, E_DOWN), (UP, W_UP, E_UP)

    def start(i):
        if i in goes_south:
            pl.when(south_ok)(rem[i].start)
        elif i in goes_north:
            pl.when(north_ok)(rem[i].start)
        else:
            rem[i].start()

    def arrived(i):
        if i in goes_south:
            pl.when(north_ok)(rem[i].wait_recv)
        elif i in goes_north:
            pl.when(south_ok)(rem[i].wait_recv)
        else:
            rem[i].wait_recv()

    def sent(i):
        if i in goes_south:
            pl.when(south_ok)(rem[i].wait_send)
        elif i in goes_north:
            pl.when(north_ok)(rem[i].wait_send)
        else:
            rem[i].wait_send()

    barrier = pltpu.get_barrier_semaphore()
    for device in (to_e, to_w):
        pl.semaphore_signal(barrier, inc=1, device_id=device, device_id_type=MESH)

    @pl.when(south_ok)
    def _():
        pl.semaphore_signal(barrier, inc=1, device_id=below, device_id_type=MESH)

    @pl.when(north_ok)
    def _():
        pl.semaphore_signal(barrier, inc=1, device_id=above, device_id_type=MESH)

    ct[ROWS:, :, :] = jnp.zeros((32 - ROWS, SIDE, D), BF)
    for strip in (wt, et):
        strip[2 * CORNER + STRIP :, :] = jnp.zeros((KEYS_S - 2 * CORNER - STRIP, D), BF)

    @pl.when(lat == 0)
    def _():
        ct[:REACH, :, :] = jnp.zeros((REACH, SIDE, D), BF)
        for strip in (wt, et):
            strip[:CORNER, :] = jnp.zeros((CORNER, D), BF)

    @pl.when(lat == n_lat - 1)
    def _():
        ct[REACH + SIDE : ROWS, :, :] = jnp.zeros((REACH, SIDE, D), BF)
        for strip in (wt, et):
            strip[CORNER + STRIP : 2 * CORNER + STRIP, :] = jnp.zeros((CORNER, D), BF)

    loc[L_TOK].wait()
    mine = ct[REACH : REACH + SIDE].reshape(SIDE * SIDE, D)
    slot, source = iota((STRIP, SIDE * SIDE), 0), iota((STRIP, SIDE * SIDE), 1)
    origin = div7(slot) * (SIDE - REACH) + slot

    def pack(offset):
        pick = jnp.where(source == origin + offset, 1.0, 0.0).astype(BF)
        return jnp.dot(pick, mine, preferred_element_type=F32).astype(BF)

    send_e[...] = pack(SIDE - REACH)
    send_w[...] = pack(0)

    @pl.when(south_ok & north_ok)
    def _():
        pl.semaphore_wait(barrier, 4)

    @pl.when(jnp.logical_not(south_ok & north_ok))
    def _():
        pl.semaphore_wait(barrier, 3)

    for i in (W_LOW, W_HIGH, DOWN, UP, E_LOW, E_HIGH):
        start(i)

    def bias(q_row, q_col, k_row, k_col):
        place = lat * SIDE + k_row
        k_row = jnp.where((place >= 0) & (place < n_lat * SIDE), k_row, 1000)
        near = (jnp.abs(k_row - q_row) <= RADIUS) & (jnp.abs(k_col - q_col) <= RADIUS)
        return jnp.where(near, 0.0, FAR)

    m = iota((2 * HALF, 1), 0)
    right = jnp.where(m >= HALF, 1, 0)
    qc_row = ((m - right * HALF) >> 3) - 1
    qc_col = (m & 7) + 8 * right
    n = iota((1, KEYS_C), 1)
    kc_row = jnp.where(n < ROWS * SIDE, (n >> 4) - REACH, 1000)
    kc_col = n & 15
    bias_c[...] = bias(qc_row, qc_col, kc_row, kc_col)
    j = iota((1, KEYS_S), 1)
    ks_row7 = div7(j + 6)
    ks_row = jnp.where(j < 2 * CORNER + STRIP, ks_row7 - 10, 1000)
    ks_col = j + 6 - 7 * ks_row7
    e = iota((EDGE, 1), 0)
    h = iota((HALF, 1), 0)
    main_row, main_col = (h >> 3) - 1, h & 7
    for side, (first_q, edge_q, first_k) in enumerate(((0, -1, -REACH), (8, SIDE, SIDE))):
        bias_s[side, :HALF, :] = bias(main_row, main_col + first_q, ks_row, ks_col + first_k)
        bias_s[side, HALF:, :] = bias(e - 1, edge_q, ks_row, ks_col + first_k)
        bias_e[side] = bias(e - 1, edge_q, kc_row, kc_col)

    lane = iota((1, INNER), 1)
    factor = jnp.zeros((1, INNER), F32)
    for head in range(HEADS):
        factor = jnp.where((lane >> 6) == head, scale[head], factor)
    block = jnp.where(
        (iota((TILE, TILE), 0) >> 6) == (iota((TILE, TILE), 1) >> 6), 1.0, 0.0
    ).astype(BF)
    first_head = (iota((1, 128), 1) < HEAD_DIM)

    for vv in (vc, vw):
        vv[:, :, 128:] = jnp.ones((PAIRS, vv.shape[1], 128), BF)

    def unit(x):
        square = x * x
        top = square.astype(BF)
        rest = (square - top.astype(F32)).astype(BF)
        total = jnp.dot(top, block, preferred_element_type=F32) + jnp.dot(
            rest, block, preferred_element_type=F32
        )
        return x * lax.rsqrt(total + 1e-06)

    def keys_values(x, rows, k_dst, v_dst):
        for t in range(2):
            cols = pl.ds(t * TILE, TILE)
            keys = jnp.dot(x, wk[:, cols], preferred_element_type=F32)
            k_dst[rows, cols] = unit(keys).astype(BF)
        for t in range(2):
            cols = pl.ds(t * TILE, TILE)
            values = jnp.dot(x, wv[:, cols], preferred_element_type=F32).astype(BF)
            v_dst[2 * t, rows, :128] = values[:, :128]
            v_dst[2 * t + 1, rows, :128] = values[:, 128:]

    def attend(q, rows, k_src, v_src, bias_ref, take):
        count = q.shape[0]
        for p in range(PAIRS):
            cols = pl.ds(128 * p, 128)
            qp = q[:, 128 * p : 128 * p + 128]
            zero = jnp.zeros_like(qp)
            both = jnp.concatenate(
                [jnp.where(first_head, qp, zero), jnp.where(first_head, zero, qp)], 0
            )
            scores = lax.dot_general(
                both, k_src[:, cols], (((1,), (1,)), ((), ())), preferred_element_type=F32
            )
            term = bias_ref[...]
            weights = jnp.concatenate(
                [
                    jnp.exp(scores[:count] + term).astype(BF),
                    jnp.exp(scores[count:] + term).astype(BF),
                ],
                0,
            )
            summed = jnp.dot(weights, v_src[p], preferred_element_type=F32)
            take(
                cols,
                jnp.where(first_head, summed[:count, :128], summed[count:, :128]),
                jnp.where(first_head, summed[:count, 128:], summed[count:, 128:]),
            )

    loc[L_GA].wait()
    gain = ga[...]
    own = pl.ds(REACH * SIDE, SIDE * SIDE)
    xn[own, :] = norm_rows(mine.astype(F32), gain).astype(BF)
    loc[L_WK].wait()
    loc[L_WV].wait()
    keys_values(xn[own, :], own, kc, vc)

    for i, first, count in ((DOWN, 0, REACH), (UP, REACH + SIDE, 32 - REACH - SIDE)):
        arrived(i)
        rows = pl.ds(first * SIDE, count * SIDE)
        x = ct[first : first + count].reshape(count * SIDE, D).astype(F32)
        xn[rows, :] = norm_rows(x, gain).astype(BF)
        keys_values(xn[rows, :], rows, kc, vc)

    def halves(x):
        x = x.reshape(RING, 2, 8, x.shape[-1])
        return [x[:, s].reshape(HALF, x.shape[-1]) for s in range(2)]

    ring = pl.ds((REACH - 1) * SIDE, RING * SIDE)
    for s, part in enumerate(halves(ct[REACH - 1 : REACH + SIDE + 1].reshape(RING * SIDE, D).astype(F32))):
        xres[s * HALF : (s + 1) * HALF, :] = part
    loc[L_WQ].wait()
    for t in range(2):
        cols = pl.ds(t * TILE, TILE)
        q = jnp.dot(xn[ring, :], wq[:, cols], preferred_element_type=F32)
        q = unit(q) * factor[:, t * TILE : (t + 1) * TILE]
        for s, part in enumerate(halves(q)):
            qc[s * HALF : (s + 1) * HALF, cols] = part.astype(BF)

    arrived(W_LOW)
    start(W_DOWN)
    arrived(W_HIGH)
    start(W_UP)

    def keep(cols, num, den):
        acc_n[: 2 * HALF, cols] = num
        acc_d[: 2 * HALF, cols] = den

    attend(qc[...], None, kc, vc, bias_c, keep)

    loc[L_GF].wait()
    loc[L_TAPS].wait()
    loc[L_WO].wait()
    loc[L_WU].wait()
    edge_rows = pl.ds(2 * HALF, EDGE)

    def side_attention(side, strip):
        everything = pl.ds(0, KEYS_S)
        xs = norm_rows(strip[...].astype(F32), gain).astype(BF)
        keys_values(xs, everything, kw, vw)
        slot, source = iota((EDGE, KEYS_S), 0), iota((EDGE, KEYS_S), 1)
        first = (CORNER + REACH - 1, CORNER)[side] - REACH
        pick = jnp.where((source == slot * REACH + first) & (slot < RING), 1.0, 0.0).astype(BF)
        edge = jnp.dot(pick, strip[...], preferred_element_type=F32)
        xe = norm_rows(edge, gain).astype(BF)
        for t in range(2):
            cols = pl.ds(t * TILE, TILE)
            q = jnp.dot(xe, wq[:, cols], preferred_element_type=F32)
            qe[HALF:, cols] = (unit(q) * factor[:, t * TILE : (t + 1) * TILE]).astype(BF)
        main = pl.ds(side * HALF, HALF)
        qe[:HALF, :] = qc[main, :]

        def first_edge(cols, num, den):
            acc_n[edge_rows, cols] = num
            acc_d[edge_rows, cols] = den

        attend(qe[HALF:, :], None, kc, vc, bias_e.at[side], first_edge)

        def add(cols, num, den):
            acc_n[main, cols] += num[:HALF]
            acc_d[main, cols] += den[:HALF]
            acc_n[edge_rows, cols] += num[HALF:]
            acc_d[edge_rows, cols] += den[HALF:]

        attend(qe[...], None, kw, vw, bias_s.at[side], add)
        return edge

    def attended(rows):
        return (acc_n[rows, :] / acc_d[rows, :]).astype(BF)

    def ffn_input(att, tokens, row_of):
        stream = tokens + jnp.dot(att, wo[...], preferred_element_type=F32)
        place = lat * SIDE + row_of - 1
        inside = (place >= 0) & (place < n_lat * SIDE)
        return jnp.where(inside, norm_rows(stream, gf[...]), 0.0).astype(BF)

    def up_project(count, hid):
        @pl.loop(0, HID // TILE)
        def _(t):
            cols = pl.ds(pl.multiple_of(t * TILE, TILE), TILE)
            hidden = jnp.dot(nf[:count, :], wu[:, cols], preferred_element_type=F32)
            hid[:count, cols] = hidden.astype(BF).astype(F32)

    sub = iota((8, TILE), 0)

    def filter_half(side, hid, west_row, east_row):
        @pl.loop(0, HID // TILE)
        def _(t):
            cols = pl.ds(pl.multiple_of(t * TILE, TILE), TILE)
            tap = [[taps[a, pl.ds(b, 1), cols] for b in range(3)] for a in range(3)]
            total = [None] * RING
            for g in range(RING):
                mid = hid[g * 8 : g * 8 + 8, cols]
                w_edge, e_edge = west_row(g, cols), east_row(g, cols)
                lower = jnp.where(sub == 0, w_edge, pltpu.roll(mid, 1, 0))
                upper = jnp.where(sub == 7, e_edge, pltpu.roll(mid, 7, 0))
                for a in range(3):
                    r = g - a
                    if 0 <= r < SIDE:
                        term = lower * tap[a][0] + mid * tap[a][1] + upper * tap[a][2]
                        total[r] = term if total[r] is None else total[r] + term
                if g >= 2:
                    r = g - 2
                    ob[r, side * 8 : side * 8 + 8, cols] = gelu(total[r]).astype(BF)

    arrived(W_DOWN)
    arrived(W_UP)
    edge = side_attention(0, wt)
    nf[:HALF, :] = ffn_input(attended(pl.ds(0, HALF)), xres[:HALF, :], h >> 3)
    nf[HALF : HALF + EDGE, :] = ffn_input(attended(edge_rows), edge, e)
    slot, source = iota((EDGE, HALF), 0), iota((EDGE, HALF), 1)
    pick = jnp.where((source == slot * 8) & (slot < RING), 1.0, 0.0).astype(BF)
    att = (acc_n[HALF : 2 * HALF, :] / acc_d[HALF : 2 * HALF, :]).astype(BF)
    att = jnp.dot(pick, att, preferred_element_type=F32).astype(BF)
    slot, source = iota((EDGE, KEYS_C), 0), iota((EDGE, KEYS_C), 1)
    pick = (source == (slot + REACH - 1) * SIDE + 8) & (slot < RING)
    pick = jnp.where(pick, 1.0, 0.0).astype(BF)
    tokens = jnp.dot(pick, ct[...].reshape(KEYS_C, D), preferred_element_type=F32)
    nf[HALF + EDGE :, :] = ffn_input(att, tokens, e)

    arrived(E_LOW)
    start(E_DOWN)
    up_project(HALF + 2 * EDGE, hid_l)
    arrived(E_HIGH)
    start(E_UP)
    filter_half(
        0, hid_l,
        lambda g, cols: hid_l[HALF + g : HALF + g + 1, cols],
        lambda g, cols: hid_l[HALF + EDGE + g : HALF + EDGE + g + 1, cols],
    )

    arrived(E_DOWN)
    arrived(E_UP)
    edge = side_attention(1, et)
    nf[:HALF, :] = ffn_input(attended(pl.ds(HALF, HALF)), xres[HALF : 2 * HALF, :], h >> 3)
    nf[HALF : HALF + EDGE, :] = ffn_input(attended(edge_rows), edge, e)
    up_project(HALF + EDGE, hid_r)
    filter_half(
        1, hid_r,
        lambda g, cols: hid_l[g * 8 + 7 : g * 8 + 8, cols],
        lambda g, cols: hid_r[HALF + g : HALF + g + 1, cols],
    )
    done = pltpu.make_async_copy(ob, out, osem.at[0])
    done.start()
    for i in range(len(rem)):
        sent(i)
    done.wait()


def on_device(tokens, gain_attn, w_qkv, logit_scale, w_out, gain_ffn, w_up, conv_taps):
    vm = pltpu.VMEM
    anywhere = pl.BlockSpec(memory_space=pl.ANY)
    return pl.pallas_call(
        kernel,
        out_shape=jax.ShapeDtypeStruct((SIDE, SIDE, HID), BF),
        in_specs=[anywhere] * 3 + [pl.BlockSpec(memory_space=pltpu.SMEM)] + [anywhere] * 4,
        out_specs=anywhere,
        scratch_shapes=[
            vm((32, SIDE, D), BF),
            vm((KEYS_S, D), BF),
            vm((KEYS_S, D), BF),
            vm((KEYS_C, D), BF),
            vm((STRIP, D), BF),
            vm((STRIP, D), BF),
            vm((D, INNER), BF),
            vm((D, INNER), BF),
            vm((D, INNER), BF),
            vm((INNER, D), BF),
            vm((D, HID), BF),
            vm((1, D), F32),
            vm((1, D), F32),
            vm((3, 3, HID), F32),
            vm((KEYS_C, INNER), BF),
            vm((PAIRS, KEYS_C, 256), BF),
            vm((KEYS_S, INNER), BF),
            vm((PAIRS, KEYS_S, 256), BF),
            vm((2 * HALF, INNER), BF),
            vm((HALF + EDGE, INNER), BF),
            vm((2 * HALF, D), F32),
            vm((2 * HALF + EDGE, INNER), F32),
            vm((2 * HALF + EDGE, INNER), F32),
            vm((2 * HALF, KEYS_C), F32),
            vm((2, HALF + EDGE, KEYS_S), F32),
            vm((2, EDGE, KEYS_C), F32),
            vm((HALF + 2 * EDGE, D), BF),
            vm((HALF + 2 * EDGE, HID), F32),
            vm((HALF + EDGE, HID), F32),
            vm((SIDE, SIDE, HID), BF),
            pltpu.SemaphoreType.DMA((9,)),
            pltpu.SemaphoreType.DMA((2,)),
            pltpu.SemaphoreType.DMA((10,)),
            pltpu.SemaphoreType.DMA((10,)),
        ],
        compiler_params=pltpu.CompilerParams(
            collective_id=0, has_side_effects=True, vmem_limit_bytes=60 * 2**20
        ),
        name="weather_block",
    )(
        tokens, gain_attn.reshape(1, D), w_qkv, logit_scale, w_out,
        gain_ffn.reshape(1, D), w_up, conv_taps,
    )


def solution(mesh):
    in_specs = (P("lat", "lon", None), P(), P(), P(), P(), P(), P(), P())
    return jax.shard_map(
        on_device, mesh=mesh, in_specs=in_specs, out_specs=P("lat", "lon", None), check_vma=False
    )
```

```python
import functools

import jax
import jax.numpy as jnp
from jax import lax
from jax.experimental import pallas as pl
from jax.experimental.pallas import tpu as pltpu
from jax.sharding import PartitionSpec as P

D = 1024
HEADS = 8
HEAD_DIM = 64
HID = 2048
RADIUS = 6
INNER = 512

SIDE = 16
REACH = RADIUS + 1
ROWS = SIDE + 2 * REACH
RING = SIDE + 2
HALF = RING * 8
EDGE = 32
STRIP = SIDE * REACH
CORNER = 64
CUT = STRIP - CORNER
KEYS_C = 512
KEYS_S = 256
PAIRS = HEADS // 2
TILE = 256
BF = jnp.bfloat16
F32 = jnp.float32
MESH = pl.DeviceIdType.MESH
FAR = -1e30

DOWN, UP, W_LOW, W_HIGH, E_LOW, E_HIGH, W_DOWN, W_UP, E_DOWN, E_UP = range(10)
L_TOK, L_GA, L_GF, L_TAPS, L_WK, L_WV, L_WQ, L_WO, L_WU = range(9)


def iota(shape, dim):
    return lax.broadcasted_iota(jnp.int32, shape, dim)


def div7(n):
    return (n * 9363) >> 16


def norm_rows(x, gain):
    centre = jnp.mean(x, -1, keepdims=True)
    moved = x - centre
    spread = jnp.mean(moved * moved, -1, keepdims=True)
    return moved * lax.rsqrt(spread + 1e-05) * gain


def gelu(x):
    size = jnp.abs(x)
    t = 1.0 / (1.0 + size * (0.3275911 * 0.7071067811865476))
    poly = 0.5 * 1.061405429
    for c in (-1.453152027, 1.421413741, -0.284496736, 0.254829592):
        poly = poly * t + 0.5 * c
    tail = poly * t * jnp.exp(x * x * -0.5)
    return jnp.maximum(x, 0.0) - size * tail


def kernel(
    tok, ga_h, wqkv_h, scale, wo_h, gf_h, wu_h, taps_h, out,
    ct, wt, et, xn, send_e, send_w, wk, wv, wq, wo, wu, ga, gf, taps,
    kc, vc, kw, vw, qc, qe, xres, acc_n, acc_d, bias_c, bias_s, bias_e,
    nf, hid_l, hid_r, ob, lsem, osem, ss, rs,
):
    lat, lon = lax.axis_index("lat"), lax.axis_index("lon")
    n_lat, n_lon = lax.axis_size("lat"), lax.axis_size("lon")
    east, west = lax.rem(lon + 1, n_lon), lax.rem(lon + n_lon - 1, n_lon)
    north_ok, south_ok = lat > 0, lat < n_lat - 1

    loc = [
        pltpu.make_async_copy(s, d, lsem.at[i])
        for i, (s, d) in enumerate((
            (tok, ct.at[pl.ds(REACH, SIDE)]),
            (ga_h, ga), (gf_h, gf), (taps_h, taps),
            (wqkv_h.at[:, pl.ds(INNER, INNER)], wk),
            (wqkv_h.at[:, pl.ds(2 * INNER, INNER)], wv),
            (wqkv_h.at[:, pl.ds(0, INNER)], wq),
            (wo_h, wo), (wu_h, wu),
        ))
    ]
    for c in loc:
        c.start()

    def remote(i, src, dst, device):
        return pltpu.make_async_remote_copy(
            src_ref=src, dst_ref=dst, send_sem=ss.at[i], recv_sem=rs.at[i],
            device_id=device, device_id_type=MESH,
        )

    below, above = (lat + 1, lon), (lat - 1, lon)
    to_e, to_w = (lat, east), (lat, west)
    low, high = pl.ds(CUT, CORNER), pl.ds(0, CUT)
    low_d, high_d = pl.ds(CORNER + CUT, CORNER), pl.ds(CORNER, CUT)
    top_d, bot_d = pl.ds(0, CORNER), pl.ds(CORNER + STRIP, CORNER)
    first_d = pl.ds(CORNER, CORNER)
    rem = [
        remote(DOWN, tok.at[pl.ds(SIDE - REACH, REACH)], ct.at[pl.ds(0, REACH)], below),
        remote(UP, tok.at[pl.ds(0, REACH)], ct.at[pl.ds(REACH + SIDE, REACH)], above),
        remote(W_LOW, send_e.at[low], wt.at[low_d], to_e),
        remote(W_HIGH, send_e.at[high], wt.at[high_d], to_e),
        remote(E_LOW, send_w.at[low], et.at[low_d], to_w),
        remote(E_HIGH, send_w.at[high], et.at[high_d], to_w),
        remote(W_DOWN, wt.at[low_d], wt.at[top_d], below),
        remote(W_UP, wt.at[first_d], wt.at[bot_d], above),
        remote(E_DOWN, et.at[low_d], et.at[top_d], below),
        remote(E_UP, et.at[first_d], et.at[bot_d], above),
    ]
    goes_south, goes_north = (DOWN, W_DOWN, E_DOWN), (UP, W_UP, E_UP)

    def start(i):
        if i in goes_south:
            pl.when(south_ok)(rem[i].start)
        elif i in goes_north:
            pl.when(north_ok)(rem[i].start)
        else:
            rem[i].start()

    def arrived(i):
        if i in goes_south:
            pl.when(north_ok)(rem[i].wait_recv)
        elif i in goes_north:
            pl.when(south_ok)(rem[i].wait_recv)
        else:
            rem[i].wait_recv()

    def sent(i):
        if i in goes_south:
            pl.when(south_ok)(rem[i].wait_send)
        elif i in goes_north:
            pl.when(north_ok)(rem[i].wait_send)
        else:
            rem[i].wait_send()

    barrier = pltpu.get_barrier_semaphore()
    for device in (to_e, to_w):
        pl.semaphore_signal(barrier, inc=1, device_id=device, device_id_type=MESH)

    @pl.when(south_ok)
    def _():
        pl.semaphore_signal(barrier, inc=1, device_id=below, device_id_type=MESH)

    @pl.when(north_ok)
    def _():
        pl.semaphore_signal(barrier, inc=1, device_id=above, device_id_type=MESH)

    ct[ROWS:, :, :] = jnp.zeros((32 - ROWS, SIDE, D), BF)
    for strip in (wt, et):
        strip[2 * CORNER + STRIP :, :] = jnp.zeros((KEYS_S - 2 * CORNER - STRIP, D), BF)

    @pl.when(lat == 0)
    def _():
        ct[:REACH, :, :] = jnp.zeros((REACH, SIDE, D), BF)
        for strip in (wt, et):
            strip[:CORNER, :] = jnp.zeros((CORNER, D), BF)

    @pl.when(lat == n_lat - 1)
    def _():
        ct[REACH + SIDE : ROWS, :, :] = jnp.zeros((REACH, SIDE, D), BF)
        for strip in (wt, et):
            strip[CORNER + STRIP : 2 * CORNER + STRIP, :] = jnp.zeros((CORNER, D), BF)

    loc[L_TOK].wait()
    mine = ct[REACH : REACH + SIDE].reshape(SIDE * SIDE, D)
    slot, source = iota((STRIP, SIDE * SIDE), 0), iota((STRIP, SIDE * SIDE), 1)
    origin = div7(slot) * (SIDE - REACH) + slot

    def pack(offset):
        pick = jnp.where(source == origin + offset, 1.0, 0.0).astype(BF)
        return jnp.dot(pick, mine, preferred_element_type=F32).astype(BF)

    send_e[...] = pack(SIDE - REACH)
    send_w[...] = pack(0)

    @pl.when(south_ok & north_ok)
    def _():
        pl.semaphore_wait(barrier, 4)

    @pl.when(jnp.logical_not(south_ok & north_ok))
    def _():
        pl.semaphore_wait(barrier, 3)

    start(DOWN)
    start(UP)
    late = lon == n_lon - 1

    @pl.when(late)
    def _():
        for i in (W_LOW, W_HIGH, E_LOW, E_HIGH):
            start(i)

    @pl.when(jnp.logical_not(late))
    def _():
        for i in (E_LOW, E_HIGH, W_LOW, W_HIGH):
            start(i)

    def follow(i):
        pl.when(jnp.logical_not(late))(lambda: start(i))

    def bias(q_row, q_col, k_row, k_col):
        place = lat * SIDE + k_row
        k_row = jnp.where((place >= 0) & (place < n_lat * SIDE), k_row, 1000)
        near = (jnp.abs(k_row - q_row) <= RADIUS) & (jnp.abs(k_col - q_col) <= RADIUS)
        return jnp.where(near, 0.0, FAR)

    m = iota((2 * HALF, 1), 0)
    right = jnp.where(m >= HALF, 1, 0)
    qc_row = ((m - right * HALF) >> 3) - 1
    qc_col = (m & 7) + 8 * right
    n = iota((1, KEYS_C), 1)
    kc_row = jnp.where(n < ROWS * SIDE, (n >> 4) - REACH, 1000)
    kc_col = n & 15
    bias_c[...] = bias(qc_row, qc_col, kc_row, kc_col)
    j = iota((1, KEYS_S), 1)
    ks_row7 = div7(j + 6)
    ks_row = jnp.where(j < 2 * CORNER + STRIP, ks_row7 - 10, 1000)
    ks_col = j + 6 - 7 * ks_row7
    e = iota((EDGE, 1), 0)
    h = iota((HALF, 1), 0)
    main_row, main_col = (h >> 3) - 1, h & 7
    for side, (first_q, edge_q, first_k) in enumerate(((0, -1, -REACH), (8, SIDE, SIDE))):
        bias_s[side, :HALF, :] = bias(main_row, main_col + first_q, ks_row, ks_col + first_k)
        bias_s[side, HALF:, :] = bias(e - 1, edge_q, ks_row, ks_col + first_k)
        bias_e[side] = bias(e - 1, edge_q, kc_row, kc_col)

    lane = iota((1, INNER), 1)
    factor = jnp.zeros((1, INNER), F32)
    for head in range(HEADS):
        factor = jnp.where((lane >> 6) == head, scale[head], factor)
    block = jnp.where(
        (iota((TILE, TILE), 0) >> 6) == (iota((TILE, TILE), 1) >> 6), 1.0, 0.0
    ).astype(BF)
    first_head = (iota((1, 128), 1) < HEAD_DIM)

    for vv in (vc, vw):
        vv[:, :, 128:] = jnp.ones((PAIRS, vv.shape[1], 128), BF)

    def unit(x):
        square = x * x
        top = square.astype(BF)
        rest = (square - top.astype(F32)).astype(BF)
        totals = []
        for t in range(INNER // TILE):
            cols = slice(t * TILE, (t + 1) * TILE)
            totals.append(
                jnp.dot(top[:, cols], block, preferred_element_type=F32)
                + jnp.dot(rest[:, cols], block, preferred_element_type=F32)
            )
        return x * lax.rsqrt(jnp.concatenate(totals, 1) + 1e-06)

    def keys_values(x, pieces, k_dst, v_dst):
        keys = jnp.dot(x, wk[...], preferred_element_type=F32)
        values = jnp.dot(x, wv[...], preferred_element_type=F32).astype(BF)
        keys = unit(keys).astype(BF)
        for first, start_row, count in pieces:
            k_dst[start_row : start_row + count, :] = keys[first : first + count]
            for p in range(PAIRS):
                v_dst[p, start_row : start_row + count, :128] = values[
                    first : first + count, 128 * p : 128 * p + 128
                ]

    def attend(q, k_src, v_src, bias_ref, take):
        count = q.shape[0]
        scores = []
        for p in range(PAIRS):
            qp = q[:, 128 * p : 128 * p + 128]
            zero = jnp.zeros_like(qp)
            both = jnp.concatenate(
                [jnp.where(first_head, qp, zero), jnp.where(first_head, zero, qp)], 0
            )
            scores.append(lax.dot_general(
                both, k_src[:, 128 * p : 128 * p + 128], (((1,), (1,)), ((), ())),
                preferred_element_type=F32,
            ))
        term = bias_ref[...]
        for p in range(PAIRS):
            weights = jnp.concatenate(
                [
                    jnp.exp(scores[p][:count] + term).astype(BF),
                    jnp.exp(scores[p][count:] + term).astype(BF),
                ],
                0,
            )
            summed = jnp.dot(weights, v_src[p], preferred_element_type=F32)
            take(
                slice(128 * p, 128 * p + 128),
                jnp.where(first_head, summed[:count, :128], summed[count:, :128]),
                jnp.where(first_head, summed[:count, 128:], summed[count:, 128:]),
            )

    loc[L_GA].wait()
    gain = ga[...]
    own = REACH * SIDE
    xn[own : own + SIDE * SIDE, :] = norm_rows(mine.astype(F32), gain).astype(BF)
    loc[L_WK].wait()
    loc[L_WV].wait()
    keys_values(xn[own : own + SIDE * SIDE, :], ((0, own, SIDE * SIDE),), kc, vc)

    arrived(DOWN)
    arrived(UP)
    tail_rows = (32 - REACH - SIDE) * SIDE
    tail = own + SIDE * SIDE
    x = jnp.concatenate(
        [
            ct[:REACH].reshape(own, D).astype(F32),
            ct[REACH + SIDE :].reshape(tail_rows, D).astype(F32),
        ],
        0,
    )
    x = norm_rows(x, gain).astype(BF)
    xn[:own, :] = x[:own]
    xn[tail:, :] = x[own:]
    keys_values(x, ((0, 0, own), (own, tail, tail_rows)), kc, vc)
    arrived(E_LOW)
    start(E_DOWN)

    def halves(x):
        x = x.reshape(RING, 2, 8, x.shape[-1])
        return [x[:, s].reshape(HALF, x.shape[-1]) for s in range(2)]

    ring = pl.ds((REACH - 1) * SIDE, RING * SIDE)
    for s, part in enumerate(halves(ct[REACH - 1 : REACH + SIDE + 1].reshape(RING * SIDE, D).astype(F32))):
        xres[s * HALF : (s + 1) * HALF, :] = part
    loc[L_WQ].wait()
    q = unit(jnp.dot(xn[ring, :], wq[...], preferred_element_type=F32)) * factor
    for s, part in enumerate(halves(q)):
        qc[s * HALF : (s + 1) * HALF, :] = part.astype(BF)

    def keep(cols, num, den):
        acc_n[: 2 * HALF, cols] = num
        acc_d[: 2 * HALF, cols] = den

    arrived(E_HIGH)
    start(E_UP)
    attend(qc[...], kc, vc, bias_c, keep)

    edge_rows = slice(2 * HALF, 2 * HALF + EDGE)
    strip_end = CORNER + STRIP

    def side_middle(strip):
        x = norm_rows(strip[CORNER:strip_end, :].astype(F32), gain).astype(BF)
        keys_values(x, ((0, CORNER, STRIP),), kw, vw)

    def side_attention(side, strip):
        last = KEYS_S - strip_end
        slot, source = iota((EDGE, KEYS_S), 0), iota((EDGE, KEYS_S), 1)
        first = (CORNER + REACH - 1, CORNER)[side] - REACH
        pick = jnp.where((source == slot * REACH + first) & (slot < RING), 1.0, 0.0).astype(BF)
        edge = jnp.dot(pick, strip[...], preferred_element_type=F32)
        x = jnp.concatenate([strip[:CORNER, :], strip[strip_end:, :]], 0).astype(F32)
        x = norm_rows(x, gain).astype(BF)
        keys_values(x, ((0, 0, CORNER), (CORNER, strip_end, last)), kw, vw)
        xe = norm_rows(edge, gain).astype(BF)
        q = unit(jnp.dot(xe, wq[...], preferred_element_type=F32)) * factor
        qe[HALF:, :] = q.astype(BF)
        main = slice(side * HALF, side * HALF + HALF)
        qe[:HALF, :] = qc[main, :]

        def first_edge(cols, num, den):
            acc_n[edge_rows, cols] = num
            acc_d[edge_rows, cols] = den

        attend(qe[HALF:, :], kc, vc, bias_e.at[side], first_edge)

        def add(cols, num, den):
            acc_n[main, cols] += num[:HALF]
            acc_d[main, cols] += den[:HALF]
            acc_n[edge_rows, cols] += num[HALF:]
            acc_d[edge_rows, cols] += den[HALF:]

        attend(qe[...], kw, vw, bias_s.at[side], add)
        return edge

    def attended(rows):
        return (acc_n[rows, :] / acc_d[rows, :]).astype(BF)

    def ffn_input(att, tokens, row_of):
        stream = tokens + jnp.dot(att, wo[...], preferred_element_type=F32)
        place = lat * SIDE + row_of - 1
        inside = (place >= 0) & (place < n_lat * SIDE)
        return jnp.where(inside, norm_rows(stream, gf[...]), 0.0).astype(BF)

    def up_project(count, hid):
        for t in range(HID // 512):
            cols = slice(t * 512, (t + 1) * 512)
            hidden = jnp.dot(nf[:count, :], wu[:, cols], preferred_element_type=F32)
            hid[:count, cols] = hidden.astype(BF).astype(F32)

    sub = iota((8, TILE), 0)

    def block_out(t):
        cols = pl.ds(pl.multiple_of(t * TILE, TILE), TILE)
        return pltpu.make_async_copy(ob.at[:, :, cols], out.at[:, :, cols], osem.at[t])

    def filter_half(side, hid, west_row, east_row, write):
        @pl.loop(0, HID // TILE)
        def _(t):
            cols = pl.ds(pl.multiple_of(t * TILE, TILE), TILE)
            tap = [[taps[a, pl.ds(b, 1), cols] for b in range(3)] for a in range(3)]
            total = [None] * RING
            for g in range(RING):
                mid = hid[g * 8 : g * 8 + 8, cols]
                w_edge, e_edge = west_row(g, cols), east_row(g, cols)
                lower = jnp.where(sub == 0, w_edge, pltpu.roll(mid, 1, 0))
                upper = jnp.where(sub == 7, e_edge, pltpu.roll(mid, 7, 0))
                for a in range(3):
                    r = g - a
                    if 0 <= r < SIDE:
                        term = lower * tap[a][0] + mid * tap[a][1] + upper * tap[a][2]
                        total[r] = term if total[r] is None else total[r] + term
                if g >= 2:
                    r = g - 2
                    ob[r, side * 8 : side * 8 + 8, cols] = gelu(total[r]).astype(BF)
            if write:
                block_out(t).start()

    side_middle(et)
    arrived(E_DOWN)
    arrived(E_UP)
    edge = side_attention(1, et)
    arrived(W_LOW)
    start(W_DOWN)
    arrived(W_HIGH)
    start(W_UP)
    loc[L_GF].wait()
    loc[L_TAPS].wait()
    loc[L_WO].wait()
    loc[L_WU].wait()
    nf[:HALF, :] = ffn_input(attended(slice(HALF, 2 * HALF)), xres[HALF:, :], h >> 3)
    nf[HALF : HALF + EDGE, :] = ffn_input(attended(edge_rows), edge, e)
    slot, source = iota((EDGE, HALF), 0), iota((EDGE, HALF), 1)
    pick = jnp.where((source == slot * 8 + 7) & (slot < RING), 1.0, 0.0).astype(BF)
    att = jnp.dot(pick, attended(slice(0, HALF)), preferred_element_type=F32).astype(BF)
    slot, source = iota((EDGE, KEYS_C), 0), iota((EDGE, KEYS_C), 1)
    pick = (source == (slot + REACH - 1) * SIDE + 7) & (slot < RING)
    pick = jnp.where(pick, 1.0, 0.0).astype(BF)
    tokens = jnp.dot(pick, ct[...].reshape(KEYS_C, D), preferred_element_type=F32)
    nf[HALF + EDGE :, :] = ffn_input(att, tokens, e)

    up_project(HALF + 2 * EDGE, hid_r)
    side_middle(wt)
    filter_half(
        1, hid_r,
        lambda g, cols: hid_r[HALF + EDGE + g : HALF + EDGE + g + 1, cols],
        lambda g, cols: hid_r[HALF + g : HALF + g + 1, cols],
        False,
    )

    arrived(W_DOWN)
    arrived(W_UP)
    edge = side_attention(0, wt)
    nf[:HALF, :] = ffn_input(attended(slice(0, HALF)), xres[:HALF, :], h >> 3)
    nf[HALF : HALF + EDGE, :] = ffn_input(attended(edge_rows), edge, e)
    up_project(HALF + EDGE, hid_l)
    filter_half(
        0, hid_l,
        lambda g, cols: hid_l[HALF + g : HALF + g + 1, cols],
        lambda g, cols: hid_r[g * 8 : g * 8 + 1, cols],
        True,
    )
    for i in range(len(rem)):
        sent(i)
    for t in range(HID // TILE):
        block_out(t).wait()


def on_device(tokens, gain_attn, w_qkv, logit_scale, w_out, gain_ffn, w_up, conv_taps):
    vm = pltpu.VMEM
    anywhere = pl.BlockSpec(memory_space=pl.ANY)
    return pl.pallas_call(
        kernel,
        out_shape=jax.ShapeDtypeStruct((SIDE, SIDE, HID), BF),
        in_specs=[anywhere] * 3 + [pl.BlockSpec(memory_space=pltpu.SMEM)] + [anywhere] * 4,
        out_specs=anywhere,
        scratch_shapes=[
            vm((32, SIDE, D), BF),
            vm((KEYS_S, D), BF),
            vm((KEYS_S, D), BF),
            vm((KEYS_C, D), BF),
            vm((STRIP, D), BF),
            vm((STRIP, D), BF),
            vm((D, INNER), BF),
            vm((D, INNER), BF),
            vm((D, INNER), BF),
            vm((INNER, D), BF),
            vm((D, HID), BF),
            vm((1, D), F32),
            vm((1, D), F32),
            vm((3, 3, HID), F32),
            vm((KEYS_C, INNER), BF),
            vm((PAIRS, KEYS_C, 256), BF),
            vm((KEYS_S, INNER), BF),
            vm((PAIRS, KEYS_S, 256), BF),
            vm((2 * HALF, INNER), BF),
            vm((HALF + EDGE, INNER), BF),
            vm((2 * HALF, D), F32),
            vm((2 * HALF + EDGE, INNER), F32),
            vm((2 * HALF + EDGE, INNER), F32),
            vm((2 * HALF, KEYS_C), F32),
            vm((2, HALF + EDGE, KEYS_S), F32),
            vm((2, EDGE, KEYS_C), F32),
            vm((HALF + 2 * EDGE, D), BF),
            vm((HALF + EDGE, HID), F32),
            vm((HALF + 2 * EDGE, HID), F32),
            vm((SIDE, SIDE, HID), BF),
            pltpu.SemaphoreType.DMA((9,)),
            pltpu.SemaphoreType.DMA((HID // TILE,)),
            pltpu.SemaphoreType.DMA((10,)),
            pltpu.SemaphoreType.DMA((10,)),
        ],
        compiler_params=pltpu.CompilerParams(
            collective_id=0, has_side_effects=True, vmem_limit_bytes=60 * 2**20
        ),
        name="weather_block",
    )(
        tokens, gain_attn.reshape(1, D), w_qkv, logit_scale, w_out,
        gain_ffn.reshape(1, D), w_up, conv_taps,
    )


def solution(mesh):
    in_specs = (P("lat", "lon", None), P(), P(), P(), P(), P(), P(), P())
    return jax.shard_map(
        on_device, mesh=mesh, in_specs=in_specs, out_specs=P("lat", "lon", None), check_vma=False
    )
```

```python
import functools

import jax
import jax.numpy as jnp
from jax import lax
from jax.experimental import pallas as pl
from jax.experimental.pallas import tpu as pltpu
from jax.sharding import PartitionSpec as P

D = 1024
HEADS = 8
HEAD_DIM = 64
HID = 2048
RADIUS = 6
INNER = 512

SIDE = 16
REACH = RADIUS + 1
ROWS = SIDE + 2 * REACH
RING = SIDE + 2
HALF = RING * 8
EDGE = 32
STRIP = SIDE * REACH
CORNER = 64
CUT = STRIP - CORNER
KEYS_C = 512
KEYS_S = 256
PAIRS = HEADS // 2
TILE = 256
BF = jnp.bfloat16
F32 = jnp.float32
MESH = pl.DeviceIdType.MESH
FAR = -1e30

DOWN, UP, W_LOW, W_HIGH, E_LOW, E_HIGH, W_DOWN, W_UP, E_DOWN, E_UP = range(10)
L_TOK, L_GA, L_GF, L_TAPS, L_WK, L_WV, L_WQ, L_WO, L_WU, L_SCALE = range(10)


def iota(shape, dim):
    return lax.broadcasted_iota(jnp.int32, shape, dim)


def div7(n):
    return (n * 9363) >> 16


def norm_rows(x, gain):
    centre = jnp.mean(x, -1, keepdims=True)
    moved = x - centre
    spread = jnp.mean(moved * moved, -1, keepdims=True)
    return moved * lax.rsqrt(spread + 1e-05) * gain


def gelu(x):
    size = jnp.abs(x)
    t = 1.0 / (1.0 + size * (0.3275911 * 0.7071067811865476))
    poly = 0.5 * 1.061405429
    for c in (-1.453152027, 1.421413741, -0.284496736, 0.254829592):
        poly = poly * t + 0.5 * c
    tail = poly * t * jnp.exp(x * x * -0.5)
    return jnp.maximum(x, 0.0) - size * tail


def kernel(
    tok, ga_h, wqkv_h, scale_h, wo_h, gf_h, wu_h, taps_h, out,
    ct, wt, et, xn, send_e, send_w, wk, wv, wq, wo, wu, ga, gf, taps,
    kc, vc, kw, vw, qc, qe, xres, acc_n, acc_d, bias_c, bias_s, bias_e,
    nf, hid_l, hid_r, scale, lsem, ss, rs,
):
    lat, lon = lax.axis_index("lat"), lax.axis_index("lon")
    n_lat, n_lon = lax.axis_size("lat"), lax.axis_size("lon")
    east, west = lax.rem(lon + 1, n_lon), lax.rem(lon + n_lon - 1, n_lon)
    north_ok, south_ok = lat > 0, lat < n_lat - 1

    loc = [
        pltpu.make_async_copy(s, d, lsem.at[i])
        for i, (s, d) in enumerate((
            (tok, ct.at[pl.ds(REACH, SIDE)]),
            (ga_h, ga), (gf_h, gf), (taps_h, taps),
            (wqkv_h.at[:, pl.ds(INNER, INNER)], wk),
            (wqkv_h.at[:, pl.ds(2 * INNER, INNER)], wv),
            (wqkv_h.at[:, pl.ds(0, INNER)], wq),
            (wo_h, wo), (wu_h, wu), (scale_h, scale),
        ))
    ]
    for c in loc:
        c.start()

    def remote(i, src, dst, device):
        return pltpu.make_async_remote_copy(
            src_ref=src, dst_ref=dst, send_sem=ss.at[i], recv_sem=rs.at[i],
            device_id=device, device_id_type=MESH,
        )

    below, above = (lat + 1, lon), (lat - 1, lon)
    to_e, to_w = (lat, east), (lat, west)
    low, high = pl.ds(CUT, CORNER), pl.ds(0, CUT)
    low_d, high_d = pl.ds(CORNER + CUT, CORNER), pl.ds(CORNER, CUT)
    top_d, bot_d = pl.ds(0, CORNER), pl.ds(CORNER + STRIP, CORNER)
    first_d = pl.ds(CORNER, CORNER)
    rem = [
        remote(DOWN, tok.at[pl.ds(SIDE - REACH, REACH)], ct.at[pl.ds(0, REACH)], below),
        remote(UP, tok.at[pl.ds(0, REACH)], ct.at[pl.ds(REACH + SIDE, REACH)], above),
        remote(W_LOW, send_e.at[low], wt.at[low_d], to_e),
        remote(W_HIGH, send_e.at[high], wt.at[high_d], to_e),
        remote(E_LOW, send_w.at[low], et.at[low_d], to_w),
        remote(E_HIGH, send_w.at[high], et.at[high_d], to_w),
        remote(W_DOWN, wt.at[low_d], wt.at[top_d], below),
        remote(W_UP, wt.at[first_d], wt.at[bot_d], above),
        remote(E_DOWN, et.at[low_d], et.at[top_d], below),
        remote(E_UP, et.at[first_d], et.at[bot_d], above),
    ]
    goes_south, goes_north = (DOWN, W_DOWN, E_DOWN), (UP, W_UP, E_UP)

    def start(i):
        if i in goes_south:
            pl.when(south_ok)(rem[i].start)
        elif i in goes_north:
            pl.when(north_ok)(rem[i].start)
        else:
            rem[i].start()

    def arrived(i):
        if i in goes_south:
            pl.when(north_ok)(rem[i].wait_recv)
        elif i in goes_north:
            pl.when(south_ok)(rem[i].wait_recv)
        else:
            rem[i].wait_recv()

    def sent(i):
        if i in goes_south:
            pl.when(south_ok)(rem[i].wait_send)
        elif i in goes_north:
            pl.when(north_ok)(rem[i].wait_send)
        else:
            rem[i].wait_send()

    barrier = pltpu.get_barrier_semaphore()
    for device in (to_e, to_w):
        pl.semaphore_signal(barrier, inc=1, device_id=device, device_id_type=MESH)

    @pl.when(south_ok)
    def _():
        pl.semaphore_signal(barrier, inc=1, device_id=below, device_id_type=MESH)

    @pl.when(north_ok)
    def _():
        pl.semaphore_signal(barrier, inc=1, device_id=above, device_id_type=MESH)

    ct[ROWS:, :, :] = jnp.zeros((32 - ROWS, SIDE, D), BF)
    for strip in (wt, et):
        strip[2 * CORNER + STRIP :, :] = jnp.zeros((KEYS_S - 2 * CORNER - STRIP, D), BF)

    @pl.when(lat == 0)
    def _():
        ct[:REACH, :, :] = jnp.zeros((REACH, SIDE, D), BF)
        for strip in (wt, et):
            strip[:CORNER, :] = jnp.zeros((CORNER, D), BF)

    @pl.when(lat == n_lat - 1)
    def _():
        ct[REACH + SIDE : ROWS, :, :] = jnp.zeros((REACH, SIDE, D), BF)
        for strip in (wt, et):
            strip[CORNER + STRIP : 2 * CORNER + STRIP, :] = jnp.zeros((CORNER, D), BF)

    loc[L_TOK].wait()
    mine = ct[REACH : REACH + SIDE].reshape(SIDE * SIDE, D)
    slot, source = iota((STRIP, SIDE * SIDE), 0), iota((STRIP, SIDE * SIDE), 1)
    origin = div7(slot) * (SIDE - REACH) + slot

    def pack(offset):
        pick = jnp.where(source == origin + offset, 1.0, 0.0).astype(BF)
        return jnp.dot(pick, mine, preferred_element_type=F32).astype(BF)

    send_e[...] = pack(SIDE - REACH)
    send_w[...] = pack(0)

    @pl.when(south_ok & north_ok)
    def _():
        pl.semaphore_wait(barrier, 4)

    @pl.when(jnp.logical_not(south_ok & north_ok))
    def _():
        pl.semaphore_wait(barrier, 3)

    start(DOWN)
    start(UP)
    late = lon == n_lon - 1

    @pl.when(late)
    def _():
        for i in (W_LOW, W_HIGH, E_LOW, E_HIGH):
            start(i)

    @pl.when(jnp.logical_not(late))
    def _():
        for i in (E_LOW, E_HIGH, W_LOW, W_HIGH):
            start(i)

    def follow(i):
        pl.when(jnp.logical_not(late))(lambda: start(i))

    def bias(q_row, q_col, k_row, k_col):
        place = lat * SIDE + k_row
        k_row = jnp.where((place >= 0) & (place < n_lat * SIDE), k_row, 1000)
        near = (jnp.abs(k_row - q_row) <= RADIUS) & (jnp.abs(k_col - q_col) <= RADIUS)
        return jnp.where(near, 0.0, FAR)

    m = iota((2 * HALF, 1), 0)
    right = jnp.where(m >= HALF, 1, 0)
    qc_row = ((m - right * HALF) >> 3) - 1
    qc_col = (m & 7) + 8 * right
    n = iota((1, KEYS_C), 1)
    kc_row = jnp.where(n < ROWS * SIDE, (n >> 4) - REACH, 1000)
    kc_col = n & 15
    bias_c[...] = bias(qc_row, qc_col, kc_row, kc_col)
    j = iota((1, KEYS_S), 1)
    ks_row7 = div7(j + 6)
    ks_row = jnp.where(j < 2 * CORNER + STRIP, ks_row7 - 10, 1000)
    ks_col = j + 6 - 7 * ks_row7
    e = iota((EDGE, 1), 0)
    h = iota((HALF, 1), 0)
    main_row, main_col = (h >> 3) - 1, h & 7
    for side, (first_q, edge_q, first_k) in enumerate(((0, -1, -REACH), (8, SIDE, SIDE))):
        bias_s[side, :HALF, :] = bias(main_row, main_col + first_q, ks_row, ks_col + first_k)
        bias_s[side, HALF:, :] = bias(e - 1, edge_q, ks_row, ks_col + first_k)
        bias_e[side] = bias(e - 1, edge_q, kc_row, kc_col)

    loc[L_SCALE].wait()
    lane = iota((1, INNER), 1)
    factor = jnp.zeros((1, INNER), F32)
    for head in range(HEADS):
        factor = jnp.where((lane >> 6) == head, scale[head], factor)
    block = jnp.where(
        (iota((TILE, TILE), 0) >> 6) == (iota((TILE, TILE), 1) >> 6), 1.0, 0.0
    ).astype(BF)
    first_head = (iota((1, 128), 1) < HEAD_DIM)

    for vv in (vc, vw):
        vv[:, :, 128:] = jnp.ones((PAIRS, vv.shape[1], 128), BF)

    def unit(x):
        square = x * x
        top = square.astype(BF)
        rest = (square - top.astype(F32)).astype(BF)
        totals = []
        for t in range(INNER // TILE):
            cols = slice(t * TILE, (t + 1) * TILE)
            totals.append(
                jnp.dot(top[:, cols], block, preferred_element_type=F32)
                + jnp.dot(rest[:, cols], block, preferred_element_type=F32)
            )
        return x * lax.rsqrt(jnp.concatenate(totals, 1) + 1e-06)

    def keys_values(x, pieces, k_dst, v_dst):
        keys = jnp.dot(x, wk[...], preferred_element_type=F32)
        values = jnp.dot(x, wv[...], preferred_element_type=F32).astype(BF)
        keys = unit(keys).astype(BF)
        for first, start_row, count in pieces:
            k_dst[start_row : start_row + count, :] = keys[first : first + count]
            for p in range(PAIRS):
                v_dst[p, start_row : start_row + count, :128] = values[
                    first : first + count, 128 * p : 128 * p + 128
                ]

    def attend(q, k_src, v_src, bias_ref, take):
        count = q.shape[0]
        scores = []
        for p in range(PAIRS):
            qp = q[:, 128 * p : 128 * p + 128]
            zero = jnp.zeros_like(qp)
            both = jnp.concatenate(
                [jnp.where(first_head, qp, zero), jnp.where(first_head, zero, qp)], 0
            )
            scores.append(lax.dot_general(
                both, k_src[:, 128 * p : 128 * p + 128], (((1,), (1,)), ((), ())),
                preferred_element_type=F32,
            ))
        term = bias_ref[...]
        for p in range(PAIRS):
            weights = jnp.concatenate(
                [
                    jnp.exp(scores[p][:count] + term).astype(BF),
                    jnp.exp(scores[p][count:] + term).astype(BF),
                ],
                0,
            )
            summed = jnp.dot(weights, v_src[p], preferred_element_type=F32)
            take(
                slice(128 * p, 128 * p + 128),
                jnp.where(first_head, summed[:count, :128], summed[count:, :128]),
                jnp.where(first_head, summed[:count, 128:], summed[count:, 128:]),
            )

    loc[L_GA].wait()
    gain = ga[...]
    own = REACH * SIDE
    xn[own : own + SIDE * SIDE, :] = norm_rows(mine.astype(F32), gain).astype(BF)
    loc[L_WK].wait()
    loc[L_WV].wait()
    keys_values(xn[own : own + SIDE * SIDE, :], ((0, own, SIDE * SIDE),), kc, vc)

    arrived(DOWN)
    arrived(UP)
    tail_rows = (32 - REACH - SIDE) * SIDE
    tail = own + SIDE * SIDE
    x = jnp.concatenate(
        [
            ct[:REACH].reshape(own, D).astype(F32),
            ct[REACH + SIDE :].reshape(tail_rows, D).astype(F32),
        ],
        0,
    )
    x = norm_rows(x, gain).astype(BF)
    xn[:own, :] = x[:own]
    xn[tail:, :] = x[own:]
    keys_values(x, ((0, 0, own), (own, tail, tail_rows)), kc, vc)
    arrived(E_LOW)
    start(E_DOWN)

    def halves(x):
        x = x.reshape(RING, 2, 8, x.shape[-1])
        return [x[:, s].reshape(HALF, x.shape[-1]) for s in range(2)]

    ring = pl.ds((REACH - 1) * SIDE, RING * SIDE)
    for s, part in enumerate(halves(ct[REACH - 1 : REACH + SIDE + 1].reshape(RING * SIDE, D).astype(F32))):
        xres[s * HALF : (s + 1) * HALF, :] = part
    loc[L_WQ].wait()
    q = unit(jnp.dot(xn[ring, :], wq[...], preferred_element_type=F32)) * factor
    for s, part in enumerate(halves(q)):
        qc[s * HALF : (s + 1) * HALF, :] = part.astype(BF)

    def keep(cols, num, den):
        acc_n[: 2 * HALF, cols] = num
        acc_d[: 2 * HALF, cols] = den

    arrived(E_HIGH)
    start(E_UP)
    attend(qc[...], kc, vc, bias_c, keep)

    edge_rows = slice(2 * HALF, 2 * HALF + EDGE)
    strip_end = CORNER + STRIP

    def side_middle(strip):
        x = norm_rows(strip[CORNER:strip_end, :].astype(F32), gain).astype(BF)
        keys_values(x, ((0, CORNER, STRIP),), kw, vw)

    def side_attention(side, strip):
        last = KEYS_S - strip_end
        slot, source = iota((EDGE, KEYS_S), 0), iota((EDGE, KEYS_S), 1)
        first = (CORNER + REACH - 1, CORNER)[side] - REACH
        pick = jnp.where((source == slot * REACH + first) & (slot < RING), 1.0, 0.0).astype(BF)
        edge = jnp.dot(pick, strip[...], preferred_element_type=F32)
        x = jnp.concatenate([strip[:CORNER, :], strip[strip_end:, :]], 0).astype(F32)
        x = norm_rows(x, gain).astype(BF)
        keys_values(x, ((0, 0, CORNER), (CORNER, strip_end, last)), kw, vw)
        xe = norm_rows(edge, gain).astype(BF)
        q = unit(jnp.dot(xe, wq[...], preferred_element_type=F32)) * factor
        qe[HALF:, :] = q.astype(BF)
        main = slice(side * HALF, side * HALF + HALF)
        qe[:HALF, :] = qc[main, :]

        def first_edge(cols, num, den):
            acc_n[edge_rows, cols] = num
            acc_d[edge_rows, cols] = den

        attend(qe[HALF:, :], kc, vc, bias_e.at[side], first_edge)

        def add(cols, num, den):
            acc_n[main, cols] += num[:HALF]
            acc_d[main, cols] += den[:HALF]
            acc_n[edge_rows, cols] += num[HALF:]
            acc_d[edge_rows, cols] += den[HALF:]

        attend(qe[...], kw, vw, bias_s.at[side], add)
        return edge

    def attended(rows):
        return (acc_n[rows, :] / acc_d[rows, :]).astype(BF)

    def ffn_input(att, tokens, row_of):
        stream = tokens + jnp.dot(att, wo[...], preferred_element_type=F32)
        place = lat * SIDE + row_of - 1
        inside = (place >= 0) & (place < n_lat * SIDE)
        return jnp.where(inside, norm_rows(stream, gf[...]), 0.0).astype(BF)

    def up_project(count, hid):
        for t in range(HID // 512):
            cols = slice(t * 512, (t + 1) * 512)
            hidden = jnp.dot(nf[:count, :], wu[:, cols], preferred_element_type=F32)
            hid[:count, cols] = hidden.astype(BF).astype(F32)

    sub = iota((8, TILE), 0)

    def filter_half(side, hid, west_row, east_row):
        @pl.loop(0, HID // TILE)
        def _(t):
            cols = pl.ds(pl.multiple_of(t * TILE, TILE), TILE)
            tap = [[taps[a, pl.ds(b, 1), cols] for b in range(3)] for a in range(3)]
            total = [None] * RING
            for g in range(RING):
                mid = hid[g * 8 : g * 8 + 8, cols]
                w_edge, e_edge = west_row(g, cols), east_row(g, cols)
                lower = jnp.where(sub == 0, w_edge, pltpu.roll(mid, 1, 0))
                upper = jnp.where(sub == 7, e_edge, pltpu.roll(mid, 7, 0))
                for a in range(3):
                    r = g - a
                    if 0 <= r < SIDE:
                        term = lower * tap[a][0] + mid * tap[a][1] + upper * tap[a][2]
                        total[r] = term if total[r] is None else total[r] + term
                if g >= 2:
                    r = g - 2
                    out[r, side * 8 : side * 8 + 8, cols] = gelu(total[r]).astype(BF)

    side_middle(et)
    arrived(E_DOWN)
    arrived(E_UP)
    edge = side_attention(1, et)
    arrived(W_LOW)
    start(W_DOWN)
    arrived(W_HIGH)
    start(W_UP)
    loc[L_GF].wait()
    loc[L_TAPS].wait()
    loc[L_WO].wait()
    loc[L_WU].wait()
    nf[:HALF, :] = ffn_input(attended(slice(HALF, 2 * HALF)), xres[HALF:, :], h >> 3)
    nf[HALF : HALF + EDGE, :] = ffn_input(attended(edge_rows), edge, e)
    slot, source = iota((EDGE, HALF), 0), iota((EDGE, HALF), 1)
    pick = jnp.where((source == slot * 8 + 7) & (slot < RING), 1.0, 0.0).astype(BF)
    att = jnp.dot(pick, attended(slice(0, HALF)), preferred_element_type=F32).astype(BF)
    slot, source = iota((EDGE, KEYS_C), 0), iota((EDGE, KEYS_C), 1)
    pick = (source == (slot + REACH - 1) * SIDE + 7) & (slot < RING)
    pick = jnp.where(pick, 1.0, 0.0).astype(BF)
    tokens = jnp.dot(pick, ct[...].reshape(KEYS_C, D), preferred_element_type=F32)
    nf[HALF + EDGE :, :] = ffn_input(att, tokens, e)

    up_project(HALF + 2 * EDGE, hid_r)
    side_middle(wt)
    filter_half(
        1, hid_r,
        lambda g, cols: hid_r[HALF + EDGE + g : HALF + EDGE + g + 1, cols],
        lambda g, cols: hid_r[HALF + g : HALF + g + 1, cols],
    )

    arrived(W_DOWN)
    arrived(W_UP)
    edge = side_attention(0, wt)
    nf[:HALF, :] = ffn_input(attended(slice(0, HALF)), xres[:HALF, :], h >> 3)
    nf[HALF : HALF + EDGE, :] = ffn_input(attended(edge_rows), edge, e)
    up_project(HALF + EDGE, hid_l)
    filter_half(
        0, hid_l,
        lambda g, cols: hid_l[HALF + g : HALF + g + 1, cols],
        lambda g, cols: hid_r[g * 8 : g * 8 + 1, cols],
    )
    for i in range(len(rem)):
        sent(i)


def on_device(tokens, gain_attn, w_qkv, logit_scale, w_out, gain_ffn, w_up, conv_taps):
    vm = pltpu.VMEM
    anywhere = pl.BlockSpec(memory_space=pl.ANY)
    return pl.pallas_call(
        kernel,
        out_shape=jax.ShapeDtypeStruct((SIDE, SIDE, HID), BF),
        in_specs=[anywhere] * 8,
        out_specs=pl.BlockSpec(memory_space=pltpu.VMEM),
        scratch_shapes=[
            vm((32, SIDE, D), BF),
            vm((KEYS_S, D), BF),
            vm((KEYS_S, D), BF),
            vm((KEYS_C, D), BF),
            vm((STRIP, D), BF),
            vm((STRIP, D), BF),
            vm((D, INNER), BF),
            vm((D, INNER), BF),
            vm((D, INNER), BF),
            vm((INNER, D), BF),
            vm((D, HID), BF),
            vm((1, D), F32),
            vm((1, D), F32),
            vm((3, 3, HID), F32),
            vm((KEYS_C, INNER), BF),
            vm((PAIRS, KEYS_C, 256), BF),
            vm((KEYS_S, INNER), BF),
            vm((PAIRS, KEYS_S, 256), BF),
            vm((2 * HALF, INNER), BF),
            vm((HALF + EDGE, INNER), BF),
            vm((2 * HALF, D), F32),
            vm((2 * HALF + EDGE, INNER), F32),
            vm((2 * HALF + EDGE, INNER), F32),
            vm((2 * HALF, KEYS_C), F32),
            vm((2, HALF + EDGE, KEYS_S), F32),
            vm((2, EDGE, KEYS_C), F32),
            vm((HALF + 2 * EDGE, D), BF),
            vm((HALF + EDGE, HID), F32),
            vm((HALF + 2 * EDGE, HID), F32),
            pltpu.SMEM((HEADS,), F32),
            pltpu.SemaphoreType.DMA((10,)),
            pltpu.SemaphoreType.DMA((10,)),
            pltpu.SemaphoreType.DMA((10,)),
        ],
        compiler_params=pltpu.CompilerParams(
            collective_id=0, has_side_effects=True, vmem_limit_bytes=52 * 2**20
        ),
        name="weather_block",
    )(
        *(pltpu.with_memory_space_constraint(x, pltpu.HBM) for x in (
            tokens, gain_attn.reshape(1, D), w_qkv, logit_scale, w_out,
            gain_ffn.reshape(1, D), w_up, conv_taps,
        ))
    )


def solution(mesh):
    in_specs = (P("lat", "lon", None), P(), P(), P(), P(), P(), P(), P())
    return jax.shard_map(
        on_device, mesh=mesh, in_specs=in_specs, out_specs=P("lat", "lon", None), check_vma=False
    )
```

```python
import functools

import jax
import jax.numpy as jnp
from jax import lax
from jax.experimental import pallas as pl
from jax.experimental.pallas import tpu as pltpu
from jax.sharding import PartitionSpec as P

D = 1024
HEADS = 8
HEAD_DIM = 64
HID = 2048
RADIUS = 6
INNER = 512

SIDE = 16
REACH = RADIUS + 1
ROWS = SIDE + 2 * REACH
RING = SIDE + 2
HALF = RING * 8
EDGE = 32
STRIP = SIDE * REACH
CORNER = 64
CUT = STRIP - CORNER
KEYS_C = 512
KEYS_S = 256
PAIRS = HEADS // 2
TILE = 256
BF = jnp.bfloat16
F32 = jnp.float32
MESH = pl.DeviceIdType.MESH
FAR = -1e30

DOWN, UP, W_LOW, W_HIGH, E_LOW, E_HIGH, W_DOWN, W_UP, E_DOWN, E_UP = range(10)
L_TOK, L_GA, L_GF, L_TAPS, L_WK, L_WV, L_WQ, L_WO, L_WU, L_SCALE = range(10)


def iota(shape, dim):
    return lax.broadcasted_iota(jnp.int32, shape, dim)


def div7(n):
    return (n * 9363) >> 16


def norm_rows(x, gain):
    centre = jnp.mean(x, -1, keepdims=True)
    moved = x - centre
    spread = jnp.mean(moved * moved, -1, keepdims=True)
    return moved * lax.rsqrt(spread + 1e-05) * gain


def gelu(x):
    size = jnp.abs(x)
    t = 1.0 / (1.0 + size * (0.3275911 * 0.7071067811865476))
    poly = 0.5 * 1.061405429
    for c in (-1.453152027, 1.421413741, -0.284496736, 0.254829592):
        poly = poly * t + 0.5 * c
    tail = poly * t * jnp.exp(x * x * -0.5)
    return jnp.maximum(x, 0.0) - size * tail


def kernel(
    tok, ga_h, wqkv_h, scale_h, wo_h, gf_h, wu_h, taps_h, out,
    ct, wt, et, xn, send_e, send_w, wk, wv, wq, wo, wu, ga, gf, taps,
    kc, vc, kw, vw, qc, qe, xres, acc_n, acc_d, bias_c, bias_s, bias_e,
    nf, hid_l, hid_r, scale, lsem, ss, rs,
):
    lat, lon = lax.axis_index("lat"), lax.axis_index("lon")
    n_lat, n_lon = lax.axis_size("lat"), lax.axis_size("lon")
    east, west = lax.rem(lon + 1, n_lon), lax.rem(lon + n_lon - 1, n_lon)
    north_ok, south_ok = lat > 0, lat < n_lat - 1

    loc = [
        pltpu.make_async_copy(s, d, lsem.at[i])
        for i, (s, d) in enumerate((
            (tok, ct.at[pl.ds(REACH, SIDE)]),
            (ga_h, ga), (gf_h, gf), (taps_h, taps),
            (wqkv_h.at[:, pl.ds(INNER, INNER)], wk),
            (wqkv_h.at[:, pl.ds(2 * INNER, INNER)], wv),
            (wqkv_h.at[:, pl.ds(0, INNER)], wq),
            (wo_h, wo), (wu_h, wu), (scale_h, scale),
        ))
    ]
    loc[L_TOK].start()

    def remote(i, src, dst, device):
        return pltpu.make_async_remote_copy(
            src_ref=src, dst_ref=dst, send_sem=ss.at[i], recv_sem=rs.at[i],
            device_id=device, device_id_type=MESH,
        )

    below, above = (lat + 1, lon), (lat - 1, lon)
    to_e, to_w = (lat, east), (lat, west)
    low, high = pl.ds(CUT, CORNER), pl.ds(0, CUT)
    low_d, high_d = pl.ds(CORNER + CUT, CORNER), pl.ds(CORNER, CUT)
    top_d, bot_d = pl.ds(0, CORNER), pl.ds(CORNER + STRIP, CORNER)
    first_d = pl.ds(CORNER, CORNER)
    rem = [
        remote(DOWN, tok.at[pl.ds(SIDE - REACH, REACH)], ct.at[pl.ds(0, REACH)], below),
        remote(UP, tok.at[pl.ds(0, REACH)], ct.at[pl.ds(REACH + SIDE, REACH)], above),
        remote(W_LOW, send_e.at[low], wt.at[low_d], to_e),
        remote(W_HIGH, send_e.at[high], wt.at[high_d], to_e),
        remote(E_LOW, send_w.at[low], et.at[low_d], to_w),
        remote(E_HIGH, send_w.at[high], et.at[high_d], to_w),
        remote(W_DOWN, wt.at[low_d], wt.at[top_d], below),
        remote(W_UP, wt.at[first_d], wt.at[bot_d], above),
        remote(E_DOWN, et.at[low_d], et.at[top_d], below),
        remote(E_UP, et.at[first_d], et.at[bot_d], above),
    ]
    seam_top, seam_bottom = lat == n_lat // 2 - 1, lat == n_lat // 2
    seam = seam_top | seam_bottom
    head = pl.ds(0, CORNER)
    direct_south = [
        remote(W_DOWN, send_e.at[low], wt.at[top_d], (lat + 1, east)),
        remote(E_DOWN, send_w.at[low], et.at[top_d], (lat + 1, west)),
    ]
    direct_north = [
        remote(W_UP, send_e.at[head], wt.at[bot_d], (lat - 1, east)),
        remote(E_UP, send_w.at[head], et.at[bot_d], (lat - 1, west)),
    ]
    goes_south, goes_north = (DOWN, W_DOWN, E_DOWN), (UP, W_UP, E_UP)

    def start(i):
        if i in (W_DOWN, E_DOWN):
            pl.when(south_ok & jnp.logical_not(seam_top))(rem[i].start)
        elif i in (W_UP, E_UP):
            pl.when(north_ok & jnp.logical_not(seam_bottom))(rem[i].start)
        elif i in goes_south:
            pl.when(south_ok)(rem[i].start)
        elif i in goes_north:
            pl.when(north_ok)(rem[i].start)
        else:
            rem[i].start()

    def arrived(i):
        if i in goes_south:
            pl.when(north_ok)(rem[i].wait_recv)
        elif i in goes_north:
            pl.when(south_ok)(rem[i].wait_recv)
        else:
            rem[i].wait_recv()

    def sent(i):
        if i in goes_south:
            pl.when(south_ok)(rem[i].wait_send)
        elif i in goes_north:
            pl.when(north_ok)(rem[i].wait_send)
        else:
            rem[i].wait_send()

    barrier = pltpu.get_barrier_semaphore()
    for device in (to_e, to_w):
        pl.semaphore_signal(barrier, inc=1, device_id=device, device_id_type=MESH)

    for there, row in ((seam_top, lat + 1), (seam_bottom, lat - 1)):

        @pl.when(there)
        def _():
            for device in ((row, east), (row, west)):
                pl.semaphore_signal(barrier, inc=1, device_id=device, device_id_type=MESH)

    @pl.when(south_ok)
    def _():
        pl.semaphore_signal(barrier, inc=1, device_id=below, device_id_type=MESH)

    @pl.when(north_ok)
    def _():
        pl.semaphore_signal(barrier, inc=1, device_id=above, device_id_type=MESH)

    loc[L_TOK].wait()
    for c in loc[1:]:
        c.start()
    mine = ct[REACH : REACH + SIDE].reshape(SIDE * SIDE, D)
    slot, source = iota((STRIP, SIDE * SIDE), 0), iota((STRIP, SIDE * SIDE), 1)
    origin = div7(slot) * (SIDE - REACH) + slot

    def pack(offset):
        pick = jnp.where(source == origin + offset, 1.0, 0.0).astype(BF)
        return jnp.dot(pick, mine, preferred_element_type=F32).astype(BF)

    send_e[...] = pack(SIDE - REACH)
    send_w[...] = pack(0)

    @pl.when(seam)
    def _():
        pl.semaphore_wait(barrier, 6)

    @pl.when(south_ok & north_ok & jnp.logical_not(seam))
    def _():
        pl.semaphore_wait(barrier, 4)

    @pl.when(jnp.logical_not(south_ok & north_ok))
    def _():
        pl.semaphore_wait(barrier, 3)

    start(DOWN)
    start(UP)
    late = lon == n_lon - 1

    @pl.when(late)
    def _():
        for i in (W_LOW, W_HIGH, E_LOW, E_HIGH):
            start(i)

    @pl.when(jnp.logical_not(late))
    def _():
        for i in (E_LOW, E_HIGH, W_LOW, W_HIGH):
            start(i)

    def follow(i):
        pl.when(jnp.logical_not(late))(lambda: start(i))

    for there, copies in ((seam_top, direct_south), (seam_bottom, direct_north)):

        @pl.when(there)
        def _():
            for copy in copies:
                copy.start()

    ct[ROWS:, :, :] = jnp.zeros((32 - ROWS, SIDE, D), BF)
    for strip in (wt, et):
        strip[2 * CORNER + STRIP :, :] = jnp.zeros((KEYS_S - 2 * CORNER - STRIP, D), BF)

    @pl.when(lat == 0)
    def _():
        ct[:REACH, :, :] = jnp.zeros((REACH, SIDE, D), BF)
        for strip in (wt, et):
            strip[:CORNER, :] = jnp.zeros((CORNER, D), BF)

    @pl.when(lat == n_lat - 1)
    def _():
        ct[REACH + SIDE : ROWS, :, :] = jnp.zeros((REACH, SIDE, D), BF)
        for strip in (wt, et):
            strip[CORNER + STRIP : 2 * CORNER + STRIP, :] = jnp.zeros((CORNER, D), BF)

    def bias(q_row, q_col, k_row, k_col):
        place = lat * SIDE + k_row
        k_row = jnp.where((place >= 0) & (place < n_lat * SIDE), k_row, 1000)
        near = (jnp.abs(k_row - q_row) <= RADIUS) & (jnp.abs(k_col - q_col) <= RADIUS)
        return jnp.where(near, 0.0, FAR)

    m = iota((2 * HALF, 1), 0)
    right = jnp.where(m >= HALF, 1, 0)
    qc_row = ((m - right * HALF) >> 3) - 1
    qc_col = (m & 7) + 8 * right
    n = iota((1, KEYS_C), 1)
    kc_row = jnp.where(n < ROWS * SIDE, (n >> 4) - REACH, 1000)
    kc_col = n & 15
    bias_c[...] = bias(qc_row, qc_col, kc_row, kc_col)
    j = iota((1, KEYS_S), 1)
    ks_row7 = div7(j + 6)
    ks_row = jnp.where(j < 2 * CORNER + STRIP, ks_row7 - 10, 1000)
    ks_col = j + 6 - 7 * ks_row7
    e = iota((EDGE, 1), 0)
    h = iota((HALF, 1), 0)
    main_row, main_col = (h >> 3) - 1, h & 7
    for side, (first_q, edge_q, first_k) in enumerate(((0, -1, -REACH), (8, SIDE, SIDE))):
        bias_s[side, :HALF, :] = bias(main_row, main_col + first_q, ks_row, ks_col + first_k)
        bias_s[side, HALF:, :] = bias(e - 1, edge_q, ks_row, ks_col + first_k)
        bias_e[side] = bias(e - 1, edge_q, kc_row, kc_col)

    loc[L_SCALE].wait()
    lane = iota((1, INNER), 1)
    factor = jnp.zeros((1, INNER), F32)
    for head in range(HEADS):
        factor = jnp.where((lane >> 6) == head, scale[head], factor)
    block = jnp.where(
        (iota((TILE, TILE), 0) >> 6) == (iota((TILE, TILE), 1) >> 6), 1.0, 0.0
    ).astype(BF)
    first_head = (iota((1, 128), 1) < HEAD_DIM)

    for vv in (vc, vw):
        vv[:, :, 128:] = jnp.ones((PAIRS, vv.shape[1], 128), BF)

    def unit(x):
        square = x * x
        top = square.astype(BF)
        rest = (square - top.astype(F32)).astype(BF)
        totals = []
        for t in range(INNER // TILE):
            cols = slice(t * TILE, (t + 1) * TILE)
            totals.append(
                jnp.dot(top[:, cols], block, preferred_element_type=F32)
                + jnp.dot(rest[:, cols], block, preferred_element_type=F32)
            )
        return x * lax.rsqrt(jnp.concatenate(totals, 1) + 1e-06)

    def keys_values(x, pieces, k_dst, v_dst):
        keys = jnp.dot(x, wk[...], preferred_element_type=F32)
        values = jnp.dot(x, wv[...], preferred_element_type=F32).astype(BF)
        keys = unit(keys).astype(BF)
        for first, start_row, count in pieces:
            k_dst[start_row : start_row + count, :] = keys[first : first + count]
            for p in range(PAIRS):
                v_dst[p, start_row : start_row + count, :128] = values[
                    first : first + count, 128 * p : 128 * p + 128
                ]

    def attend(q, k_src, v_src, bias_ref, take):
        count = q.shape[0]
        scores = []
        for p in range(PAIRS):
            qp = q[:, 128 * p : 128 * p + 128]
            zero = jnp.zeros_like(qp)
            both = jnp.concatenate(
                [jnp.where(first_head, qp, zero), jnp.where(first_head, zero, qp)], 0
            )
            scores.append(lax.dot_general(
                both, k_src[:, 128 * p : 128 * p + 128], (((1,), (1,)), ((), ())),
                preferred_element_type=F32,
            ))
        term = bias_ref[...]
        for p in range(PAIRS):
            weights = jnp.concatenate(
                [
                    jnp.exp(scores[p][:count] + term).astype(BF),
                    jnp.exp(scores[p][count:] + term).astype(BF),
                ],
                0,
            )
            summed = jnp.dot(weights, v_src[p], preferred_element_type=F32)
            take(
                slice(128 * p, 128 * p + 128),
                jnp.where(first_head, summed[:count, :128], summed[count:, :128]),
                jnp.where(first_head, summed[:count, 128:], summed[count:, 128:]),
            )

    loc[L_GA].wait()
    gain = ga[...]
    own = REACH * SIDE
    xn[own : own + SIDE * SIDE, :] = norm_rows(mine.astype(F32), gain).astype(BF)
    loc[L_WK].wait()
    loc[L_WV].wait()
    keys_values(xn[own : own + SIDE * SIDE, :], ((0, own, SIDE * SIDE),), kc, vc)

    arrived(DOWN)
    arrived(UP)
    tail_rows = (32 - REACH - SIDE) * SIDE
    tail = own + SIDE * SIDE
    x = jnp.concatenate(
        [
            ct[:REACH].reshape(own, D).astype(F32),
            ct[REACH + SIDE :].reshape(tail_rows, D).astype(F32),
        ],
        0,
    )
    x = norm_rows(x, gain).astype(BF)
    xn[:own, :] = x[:own]
    xn[tail:, :] = x[own:]
    keys_values(x, ((0, 0, own), (own, tail, tail_rows)), kc, vc)
    arrived(E_LOW)
    start(E_DOWN)

    def halves(x):
        x = x.reshape(RING, 2, 8, x.shape[-1])
        return [x[:, s].reshape(HALF, x.shape[-1]) for s in range(2)]

    ring = pl.ds((REACH - 1) * SIDE, RING * SIDE)
    for s, part in enumerate(halves(ct[REACH - 1 : REACH + SIDE + 1].reshape(RING * SIDE, D).astype(F32))):
        xres[s * HALF : (s + 1) * HALF, :] = part
    loc[L_WQ].wait()
    q = unit(jnp.dot(xn[ring, :], wq[...], preferred_element_type=F32)) * factor
    for s, part in enumerate(halves(q)):
        qc[s * HALF : (s + 1) * HALF, :] = part.astype(BF)

    def keep(cols, num, den):
        acc_n[: 2 * HALF, cols] = num
        acc_d[: 2 * HALF, cols] = den

    arrived(E_HIGH)
    start(E_UP)
    attend(qc[...], kc, vc, bias_c, keep)

    edge_rows = slice(2 * HALF, 2 * HALF + EDGE)
    strip_end = CORNER + STRIP

    def side_middle(strip):
        x = norm_rows(strip[CORNER:strip_end, :].astype(F32), gain).astype(BF)
        keys_values(x, ((0, CORNER, STRIP),), kw, vw)

    def side_attention(side, strip):
        last = KEYS_S - strip_end
        slot, source = iota((EDGE, KEYS_S), 0), iota((EDGE, KEYS_S), 1)
        first = (CORNER + REACH - 1, CORNER)[side] - REACH
        pick = jnp.where((source == slot * REACH + first) & (slot < RING), 1.0, 0.0).astype(BF)
        edge = jnp.dot(pick, strip[...], preferred_element_type=F32)
        x = jnp.concatenate([strip[:CORNER, :], strip[strip_end:, :]], 0).astype(F32)
        x = norm_rows(x, gain).astype(BF)
        keys_values(x, ((0, 0, CORNER), (CORNER, strip_end, last)), kw, vw)
        xe = norm_rows(edge, gain).astype(BF)
        q = unit(jnp.dot(xe, wq[...], preferred_element_type=F32)) * factor
        qe[HALF:, :] = q.astype(BF)
        main = slice(side * HALF, side * HALF + HALF)
        qe[:HALF, :] = qc[main, :]

        def first_edge(cols, num, den):
            acc_n[edge_rows, cols] = num
            acc_d[edge_rows, cols] = den

        attend(qe[HALF:, :], kc, vc, bias_e.at[side], first_edge)

        def add(cols, num, den):
            acc_n[main, cols] += num[:HALF]
            acc_d[main, cols] += den[:HALF]
            acc_n[edge_rows, cols] += num[HALF:]
            acc_d[edge_rows, cols] += den[HALF:]

        attend(qe[...], kw, vw, bias_s.at[side], add)
        return edge

    def attended(rows):
        return (acc_n[rows, :] / acc_d[rows, :]).astype(BF)

    def ffn_input(att, tokens, row_of):
        stream = tokens + jnp.dot(att, wo[...], preferred_element_type=F32)
        place = lat * SIDE + row_of - 1
        inside = (place >= 0) & (place < n_lat * SIDE)
        return jnp.where(inside, norm_rows(stream, gf[...]), 0.0).astype(BF)

    def up_project(count, hid):
        for t in range(HID // 512):
            cols = slice(t * 512, (t + 1) * 512)
            hidden = jnp.dot(nf[:count, :], wu[:, cols], preferred_element_type=F32)
            hid[:count, cols] = hidden.astype(BF).astype(F32)

    sub = iota((8, TILE), 0)

    def filter_half(side, hid, west_row, east_row):
        @pl.loop(0, HID // TILE)
        def _(t):
            cols = pl.ds(pl.multiple_of(t * TILE, TILE), TILE)
            tap = [[taps[a, pl.ds(b, 1), cols] for b in range(3)] for a in range(3)]
            total = [None] * RING
            for g in range(RING):
                mid = hid[g * 8 : g * 8 + 8, cols]
                w_edge, e_edge = west_row(g, cols), east_row(g, cols)
                lower = jnp.where(sub == 0, w_edge, pltpu.roll(mid, 1, 0))
                upper = jnp.where(sub == 7, e_edge, pltpu.roll(mid, 7, 0))
                for a in range(3):
                    r = g - a
                    if 0 <= r < SIDE:
                        term = lower * tap[a][0] + mid * tap[a][1] + upper * tap[a][2]
                        total[r] = term if total[r] is None else total[r] + term
                if g >= 2:
                    r = g - 2
                    out[r, side * 8 : side * 8 + 8, cols] = gelu(total[r]).astype(BF)

    side_middle(et)
    arrived(W_LOW)
    start(W_DOWN)
    arrived(E_DOWN)
    arrived(E_UP)
    edge = side_attention(1, et)
    arrived(W_HIGH)
    start(W_UP)
    loc[L_GF].wait()
    loc[L_TAPS].wait()
    loc[L_WO].wait()
    loc[L_WU].wait()
    slot, source = iota((EDGE, HALF), 0), iota((EDGE, HALF), 1)
    pick = jnp.where((source == slot * 8 + 7) & (slot < RING), 1.0, 0.0).astype(BF)
    att = jnp.dot(pick, attended(slice(0, HALF)), preferred_element_type=F32).astype(BF)
    slot, source = iota((EDGE, KEYS_C), 0), iota((EDGE, KEYS_C), 1)
    pick = (source == (slot + REACH - 1) * SIDE + 7) & (slot < RING)
    pick = jnp.where(pick, 1.0, 0.0).astype(BF)
    tokens = jnp.dot(pick, ct[...].reshape(KEYS_C, D), preferred_element_type=F32)
    nf[...] = ffn_input(
        jnp.concatenate([attended(slice(HALF, 2 * HALF + EDGE)), att], 0),
        jnp.concatenate([xres[HALF:, :], edge, tokens], 0),
        jnp.concatenate([h >> 3, e, e], 0),
    )

    up_project(HALF + 2 * EDGE, hid_r)
    side_middle(wt)
    filter_half(
        1, hid_r,
        lambda g, cols: hid_r[HALF + EDGE + g : HALF + EDGE + g + 1, cols],
        lambda g, cols: hid_r[HALF + g : HALF + g + 1, cols],
    )

    arrived(W_DOWN)
    arrived(W_UP)
    edge = side_attention(0, wt)
    nf[: HALF + EDGE, :] = ffn_input(
        jnp.concatenate([attended(slice(0, HALF)), attended(edge_rows)], 0),
        jnp.concatenate([xres[:HALF, :], edge], 0),
        jnp.concatenate([h >> 3, e], 0),
    )
    up_project(HALF + EDGE, hid_l)
    filter_half(
        0, hid_l,
        lambda g, cols: hid_l[HALF + g : HALF + g + 1, cols],
        lambda g, cols: hid_r[g * 8 : g * 8 + 1, cols],
    )
    for i in range(len(rem)):
        sent(i)


def on_device(tokens, gain_attn, w_qkv, logit_scale, w_out, gain_ffn, w_up, conv_taps):
    vm = pltpu.VMEM
    anywhere = pl.BlockSpec(memory_space=pl.ANY)
    return pl.pallas_call(
        kernel,
        out_shape=jax.ShapeDtypeStruct((SIDE, SIDE, HID), BF),
        in_specs=[anywhere] * 8,
        out_specs=pl.BlockSpec(memory_space=pltpu.VMEM),
        scratch_shapes=[
            vm((32, SIDE, D), BF),
            vm((KEYS_S, D), BF),
            vm((KEYS_S, D), BF),
            vm((KEYS_C, D), BF),
            vm((STRIP, D), BF),
            vm((STRIP, D), BF),
            vm((D, INNER), BF),
            vm((D, INNER), BF),
            vm((D, INNER), BF),
            vm((INNER, D), BF),
            vm((D, HID), BF),
            vm((1, D), F32),
            vm((1, D), F32),
            vm((3, 3, HID), F32),
            vm((KEYS_C, INNER), BF),
            vm((PAIRS, KEYS_C, 256), BF),
            vm((KEYS_S, INNER), BF),
            vm((PAIRS, KEYS_S, 256), BF),
            vm((2 * HALF, INNER), BF),
            vm((HALF + EDGE, INNER), BF),
            vm((2 * HALF, D), F32),
            vm((2 * HALF + EDGE, INNER), F32),
            vm((2 * HALF + EDGE, INNER), F32),
            vm((2 * HALF, KEYS_C), F32),
            vm((2, HALF + EDGE, KEYS_S), F32),
            vm((2, EDGE, KEYS_C), F32),
            vm((HALF + 2 * EDGE, D), BF),
            vm((HALF + EDGE, HID), F32),
            vm((HALF + 2 * EDGE, HID), F32),
            pltpu.SMEM((HEADS,), F32),
            pltpu.SemaphoreType.DMA((10,)),
            pltpu.SemaphoreType.DMA((10,)),
            pltpu.SemaphoreType.DMA((10,)),
        ],
        compiler_params=pltpu.CompilerParams(
            collective_id=0, has_side_effects=True, vmem_limit_bytes=52 * 2**20
        ),
        name="weather_block",
    )(
        *(pltpu.with_memory_space_constraint(x, pltpu.HBM) for x in (
            tokens, gain_attn.reshape(1, D), w_qkv, logit_scale, w_out,
            gain_ffn.reshape(1, D), w_up, conv_taps,
        ))
    )


def solution(mesh):
    in_specs = (P("lat", "lon", None), P(), P(), P(), P(), P(), P(), P())
    return jax.shard_map(
        on_device, mesh=mesh, in_specs=in_specs, out_specs=P("lat", "lon", None), check_vma=False
    )
```

```python
import functools

import jax
import jax.numpy as jnp
from jax import lax
from jax.experimental import pallas as pl
from jax.experimental.pallas import tpu as pltpu
from jax.sharding import PartitionSpec as P

D = 1024
HEADS = 8
HEAD_DIM = 64
HID = 2048
RADIUS = 6
INNER = 512

SIDE = 16
REACH = RADIUS + 1
ROWS = SIDE + 2 * REACH
RING = SIDE + 2
HALF = RING * 8
EDGE = 32
STRIP = SIDE * REACH
CORNER = 64
CUT = STRIP - CORNER
KEYS_C = 512
KEYS_S = 256
PAIRS = HEADS // 2
TILE = 256
BF = jnp.bfloat16
F32 = jnp.float32
MESH = pl.DeviceIdType.MESH
FAR = -1e30

DOWN, UP, W_LOW, W_HIGH, E_LOW, E_HIGH, W_DOWN, W_UP, E_DOWN, E_UP, W_UP2, E_UP2 = range(12)
L_TOK, L_GA, L_GF, L_TAPS, L_WK, L_WV, L_WQ, L_WO, L_WU, L_SCALE = range(10)


def iota(shape, dim):
    return lax.broadcasted_iota(jnp.int32, shape, dim)


def div7(n):
    return (n * 9363) >> 16


def norm_rows(x, gain):
    centre = jnp.mean(x, -1, keepdims=True)
    moved = x - centre
    spread = jnp.mean(moved * moved, -1, keepdims=True)
    return moved * lax.rsqrt(spread + 1e-05) * gain


def gelu(x):
    size = jnp.abs(x)
    t = 1.0 / (1.0 + size * (0.3275911 * 0.7071067811865476))
    poly = 0.5 * 1.061405429
    for c in (-1.453152027, 1.421413741, -0.284496736, 0.254829592):
        poly = poly * t + 0.5 * c
    tail = poly * t * jnp.exp(x * x * -0.5)
    return jnp.maximum(x, 0.0) - size * tail


def kernel(
    tok, ga_h, wqkv_h, scale_h, wo_h, gf_h, wu_h, taps_h, out,
    ct, wt, et, xn, send_e, send_w, wk, wv, wq, wo, wu, ga, gf, taps,
    kc, vc, kw, vw, qc, qe, xres, acc_n, acc_d, bias_c, bias_s, bias_e,
    nf, hid_l, hid_r, scale, lsem, ss, rs,
):
    lat, lon = lax.axis_index("lat"), lax.axis_index("lon")
    n_lat, n_lon = lax.axis_size("lat"), lax.axis_size("lon")
    east, west = lax.rem(lon + 1, n_lon), lax.rem(lon + n_lon - 1, n_lon)
    north_ok, south_ok = lat > 0, lat < n_lat - 1

    loc = [
        pltpu.make_async_copy(s, d, lsem.at[i])
        for i, (s, d) in enumerate((
            (tok, ct.at[pl.ds(REACH, SIDE)]),
            (ga_h, ga), (gf_h, gf), (taps_h, taps),
            (wqkv_h.at[:, pl.ds(INNER, INNER)], wk),
            (wqkv_h.at[:, pl.ds(2 * INNER, INNER)], wv),
            (wqkv_h.at[:, pl.ds(0, INNER)], wq),
            (wo_h, wo), (wu_h, wu), (scale_h, scale),
        ))
    ]
    loc[L_TOK].start()

    def remote(i, src, dst, device):
        return pltpu.make_async_remote_copy(
            src_ref=src, dst_ref=dst, send_sem=ss.at[i], recv_sem=rs.at[i],
            device_id=device, device_id_type=MESH,
        )

    below, above = (lat + 1, lon), (lat - 1, lon)
    to_e, to_w = (lat, east), (lat, west)
    low, high = pl.ds(CUT, CORNER), pl.ds(0, CUT)
    low_d, high_d = pl.ds(CORNER + CUT, CORNER), pl.ds(CORNER, CUT)
    top_d = pl.ds(0, CORNER)
    first_d, second_d = pl.ds(CORNER, CUT), pl.ds(CORNER + CUT, CORNER - CUT)
    bot_first = pl.ds(CORNER + STRIP, CUT)
    bot_second = pl.ds(CORNER + STRIP + CUT, CORNER - CUT)
    rem = [
        remote(DOWN, tok.at[pl.ds(SIDE - REACH, REACH)], ct.at[pl.ds(0, REACH)], below),
        remote(UP, tok.at[pl.ds(0, REACH)], ct.at[pl.ds(REACH + SIDE, REACH)], above),
        remote(W_LOW, send_e.at[low], wt.at[low_d], to_e),
        remote(W_HIGH, send_e.at[high], wt.at[high_d], to_e),
        remote(E_LOW, send_w.at[low], et.at[low_d], to_w),
        remote(E_HIGH, send_w.at[high], et.at[high_d], to_w),
        remote(W_DOWN, wt.at[low_d], wt.at[top_d], below),
        remote(W_UP, wt.at[first_d], wt.at[bot_first], above),
        remote(E_DOWN, et.at[low_d], et.at[top_d], below),
        remote(E_UP, et.at[first_d], et.at[bot_first], above),
        remote(W_UP2, wt.at[second_d], wt.at[bot_second], above),
        remote(E_UP2, et.at[second_d], et.at[bot_second], above),
    ]
    seam_top, seam_bottom = lat == n_lat // 2 - 1, lat == n_lat // 2
    seam = seam_top | seam_bottom
    head, neck = pl.ds(0, CUT), pl.ds(CUT, CORNER - CUT)
    direct_south = [
        remote(W_DOWN, send_e.at[low], wt.at[top_d], (lat + 1, east)),
        remote(E_DOWN, send_w.at[low], et.at[top_d], (lat + 1, west)),
    ]
    direct_north = [
        remote(W_UP, send_e.at[head], wt.at[bot_first], (lat - 1, east)),
        remote(E_UP, send_w.at[head], et.at[bot_first], (lat - 1, west)),
        remote(W_UP2, send_e.at[neck], wt.at[bot_second], (lat - 1, east)),
        remote(E_UP2, send_w.at[neck], et.at[bot_second], (lat - 1, west)),
    ]
    goes_south, goes_north = (DOWN, W_DOWN, E_DOWN), (UP, W_UP, E_UP, W_UP2, E_UP2)

    def start(i):
        if i in (W_DOWN, E_DOWN):
            pl.when(south_ok & jnp.logical_not(seam_top))(rem[i].start)
        elif i in (W_UP, E_UP, W_UP2, E_UP2):
            pl.when(north_ok & jnp.logical_not(seam_bottom))(rem[i].start)
        elif i in goes_south:
            pl.when(south_ok)(rem[i].start)
        elif i in goes_north:
            pl.when(north_ok)(rem[i].start)
        else:
            rem[i].start()

    def arrived(i):
        if i in goes_south:
            pl.when(north_ok)(rem[i].wait_recv)
        elif i in goes_north:
            pl.when(south_ok)(rem[i].wait_recv)
        else:
            rem[i].wait_recv()

    def sent(i):
        if i in goes_south:
            pl.when(south_ok)(rem[i].wait_send)
        elif i in goes_north:
            pl.when(north_ok)(rem[i].wait_send)
        else:
            rem[i].wait_send()

    barrier = pltpu.get_barrier_semaphore()
    for device in (to_e, to_w):
        pl.semaphore_signal(barrier, inc=1, device_id=device, device_id_type=MESH)

    for there, row in ((seam_top, lat + 1), (seam_bottom, lat - 1)):

        @pl.when(there)
        def _():
            for device in ((row, east), (row, west)):
                pl.semaphore_signal(barrier, inc=1, device_id=device, device_id_type=MESH)

    @pl.when(south_ok)
    def _():
        pl.semaphore_signal(barrier, inc=1, device_id=below, device_id_type=MESH)

    @pl.when(north_ok)
    def _():
        pl.semaphore_signal(barrier, inc=1, device_id=above, device_id_type=MESH)

    loc[L_TOK].wait()
    for c in loc[1:]:
        c.start()
    mine = ct[REACH : REACH + SIDE].reshape(SIDE * SIDE, D)
    slot, source = iota((STRIP, SIDE * SIDE), 0), iota((STRIP, SIDE * SIDE), 1)
    origin = div7(slot) * (SIDE - REACH) + slot

    def pack(offset):
        pick = jnp.where(source == origin + offset, 1.0, 0.0).astype(BF)
        return jnp.dot(pick, mine, preferred_element_type=F32).astype(BF)

    send_e[...] = pack(SIDE - REACH)
    send_w[...] = pack(0)

    @pl.when(seam)
    def _():
        pl.semaphore_wait(barrier, 6)

    @pl.when(south_ok & north_ok & jnp.logical_not(seam))
    def _():
        pl.semaphore_wait(barrier, 4)

    @pl.when(jnp.logical_not(south_ok & north_ok))
    def _():
        pl.semaphore_wait(barrier, 3)

    start(DOWN)
    start(UP)
    late = lon == n_lon - 1

    @pl.when(late)
    def _():
        for i in (W_LOW, W_HIGH, E_LOW, E_HIGH):
            start(i)

    @pl.when(jnp.logical_not(late))
    def _():
        for i in (E_LOW, E_HIGH, W_LOW, W_HIGH):
            start(i)

    def follow(i):
        pl.when(jnp.logical_not(late))(lambda: start(i))

    for there, copies in ((seam_top, direct_south), (seam_bottom, direct_north)):

        @pl.when(there)
        def _():
            for copy in copies:
                copy.start()

    ct[ROWS:, :, :] = jnp.zeros((32 - ROWS, SIDE, D), BF)
    for strip in (wt, et):
        strip[2 * CORNER + STRIP :, :] = jnp.zeros((KEYS_S - 2 * CORNER - STRIP, D), BF)

    @pl.when(lat == 0)
    def _():
        ct[:REACH, :, :] = jnp.zeros((REACH, SIDE, D), BF)
        for strip in (wt, et):
            strip[:CORNER, :] = jnp.zeros((CORNER, D), BF)

    @pl.when(lat == n_lat - 1)
    def _():
        ct[REACH + SIDE : ROWS, :, :] = jnp.zeros((REACH, SIDE, D), BF)
        for strip in (wt, et):
            strip[CORNER + STRIP : 2 * CORNER + STRIP, :] = jnp.zeros((CORNER, D), BF)

    def bias(q_row, q_col, k_row, k_col):
        place = lat * SIDE + k_row
        k_row = jnp.where((place >= 0) & (place < n_lat * SIDE), k_row, 1000)
        near = (jnp.abs(k_row - q_row) <= RADIUS) & (jnp.abs(k_col - q_col) <= RADIUS)
        return jnp.where(near, 0.0, FAR)

    m = iota((2 * HALF, 1), 0)
    right = jnp.where(m >= HALF, 1, 0)
    qc_row = ((m - right * HALF) >> 3) - 1
    qc_col = (m & 7) + 8 * right
    n = iota((1, KEYS_C), 1)
    kc_row = jnp.where(n < ROWS * SIDE, (n >> 4) - REACH, 1000)
    kc_col = n & 15
    bias_c[...] = bias(qc_row, qc_col, kc_row, kc_col)
    j = iota((1, KEYS_S), 1)
    ks_row7 = div7(j + 6)
    ks_row = jnp.where(j < 2 * CORNER + STRIP, ks_row7 - 10, 1000)
    ks_col = j + 6 - 7 * ks_row7
    e = iota((EDGE, 1), 0)
    h = iota((HALF, 1), 0)
    main_row, main_col = (h >> 3) - 1, h & 7
    for side, (first_q, edge_q, first_k) in enumerate(((0, -1, -REACH), (8, SIDE, SIDE))):
        bias_s[side, :HALF, :] = bias(main_row, main_col + first_q, ks_row, ks_col + first_k)
        bias_s[side, HALF:, :] = bias(e - 1, edge_q, ks_row, ks_col + first_k)
        bias_e[side] = bias(e - 1, edge_q, kc_row, kc_col)

    loc[L_SCALE].wait()
    lane = iota((1, INNER), 1)
    factor = jnp.zeros((1, INNER), F32)
    for head in range(HEADS):
        factor = jnp.where((lane >> 6) == head, scale[head], factor)
    block = jnp.where(
        (iota((TILE, TILE), 0) >> 6) == (iota((TILE, TILE), 1) >> 6), 1.0, 0.0
    ).astype(BF)
    first_head = (iota((1, 128), 1) < HEAD_DIM)

    for vv in (vc, vw):
        vv[:, :, 128:] = jnp.ones((PAIRS, vv.shape[1], 128), BF)

    def unit(x):
        square = x * x
        top = square.astype(BF)
        rest = (square - top.astype(F32)).astype(BF)
        totals = []
        for t in range(INNER // TILE):
            cols = slice(t * TILE, (t + 1) * TILE)
            totals.append(
                jnp.dot(top[:, cols], block, preferred_element_type=F32)
                + jnp.dot(rest[:, cols], block, preferred_element_type=F32)
            )
        return x * lax.rsqrt(jnp.concatenate(totals, 1) + 1e-06)

    def keys_values(x, pieces, k_dst, v_dst):
        keys = jnp.dot(x, wk[...], preferred_element_type=F32)
        values = jnp.dot(x, wv[...], preferred_element_type=F32).astype(BF)
        keys = unit(keys).astype(BF)
        for first, start_row, count in pieces:
            k_dst[start_row : start_row + count, :] = keys[first : first + count]
            for p in range(PAIRS):
                v_dst[p, start_row : start_row + count, :128] = values[
                    first : first + count, 128 * p : 128 * p + 128
                ]

    def attend(q, k_src, v_src, bias_ref, take):
        count = q.shape[0]
        scores = []
        for p in range(PAIRS):
            qp = q[:, 128 * p : 128 * p + 128]
            zero = jnp.zeros_like(qp)
            both = jnp.concatenate(
                [jnp.where(first_head, qp, zero), jnp.where(first_head, zero, qp)], 0
            )
            scores.append(lax.dot_general(
                both, k_src[:, 128 * p : 128 * p + 128], (((1,), (1,)), ((), ())),
                preferred_element_type=F32,
            ))
        term = bias_ref[...]
        for p in range(PAIRS):
            weights = jnp.concatenate(
                [
                    jnp.exp(scores[p][:count] + term).astype(BF),
                    jnp.exp(scores[p][count:] + term).astype(BF),
                ],
                0,
            )
            summed = jnp.dot(weights, v_src[p], preferred_element_type=F32)
            take(
                slice(128 * p, 128 * p + 128),
                jnp.where(first_head, summed[:count, :128], summed[count:, :128]),
                jnp.where(first_head, summed[:count, 128:], summed[count:, 128:]),
            )

    loc[L_GA].wait()
    gain = ga[...]
    own = REACH * SIDE
    xn[own : own + SIDE * SIDE, :] = norm_rows(mine.astype(F32), gain).astype(BF)
    loc[L_WK].wait()
    loc[L_WV].wait()
    keys_values(xn[own : own + SIDE * SIDE, :], ((0, own, SIDE * SIDE),), kc, vc)

    arrived(DOWN)
    arrived(UP)
    tail_rows = (32 - REACH - SIDE) * SIDE
    tail = own + SIDE * SIDE
    x = jnp.concatenate(
        [
            ct[:REACH].reshape(own, D).astype(F32),
            ct[REACH + SIDE :].reshape(tail_rows, D).astype(F32),
        ],
        0,
    )
    x = norm_rows(x, gain).astype(BF)
    xn[:own, :] = x[:own]
    xn[tail:, :] = x[own:]
    keys_values(x, ((0, 0, own), (own, tail, tail_rows)), kc, vc)
    arrived(E_LOW)
    start(E_DOWN)
    start(E_UP2)

    def halves(x):
        x = x.reshape(RING, 2, 8, x.shape[-1])
        return [x[:, s].reshape(HALF, x.shape[-1]) for s in range(2)]

    ring = pl.ds((REACH - 1) * SIDE, RING * SIDE)
    for s, part in enumerate(halves(ct[REACH - 1 : REACH + SIDE + 1].reshape(RING * SIDE, D).astype(F32))):
        xres[s * HALF : (s + 1) * HALF, :] = part
    loc[L_WQ].wait()
    q = unit(jnp.dot(xn[ring, :], wq[...], preferred_element_type=F32)) * factor
    for s, part in enumerate(halves(q)):
        qc[s * HALF : (s + 1) * HALF, :] = part.astype(BF)

    def keep(cols, num, den):
        acc_n[: 2 * HALF, cols] = num
        acc_d[: 2 * HALF, cols] = den

    arrived(E_HIGH)
    start(E_UP)
    attend(qc[...], kc, vc, bias_c, keep)

    edge_rows = slice(2 * HALF, 2 * HALF + EDGE)
    strip_end = CORNER + STRIP

    def side_middle(strip):
        x = norm_rows(strip[CORNER:strip_end, :].astype(F32), gain).astype(BF)
        keys_values(x, ((0, CORNER, STRIP),), kw, vw)

    def side_attention(side, strip):
        last = KEYS_S - strip_end
        slot, source = iota((EDGE, KEYS_S), 0), iota((EDGE, KEYS_S), 1)
        first = (CORNER + REACH - 1, CORNER)[side] - REACH
        pick = jnp.where((source == slot * REACH + first) & (slot < RING), 1.0, 0.0).astype(BF)
        edge = jnp.dot(pick, strip[...], preferred_element_type=F32)
        x = jnp.concatenate([strip[:CORNER, :], strip[strip_end:, :]], 0).astype(F32)
        x = norm_rows(x, gain).astype(BF)
        keys_values(x, ((0, 0, CORNER), (CORNER, strip_end, last)), kw, vw)
        xe = norm_rows(edge, gain).astype(BF)
        q = unit(jnp.dot(xe, wq[...], preferred_element_type=F32)) * factor
        qe[HALF:, :] = q.astype(BF)
        main = slice(side * HALF, side * HALF + HALF)
        qe[:HALF, :] = qc[main, :]

        def first_edge(cols, num, den):
            acc_n[edge_rows, cols] = num
            acc_d[edge_rows, cols] = den

        attend(qe[HALF:, :], kc, vc, bias_e.at[side], first_edge)

        def add(cols, num, den):
            acc_n[main, cols] += num[:HALF]
            acc_d[main, cols] += den[:HALF]
            acc_n[edge_rows, cols] += num[HALF:]
            acc_d[edge_rows, cols] += den[HALF:]

        attend(qe[...], kw, vw, bias_s.at[side], add)
        return edge

    def attended(rows):
        return (acc_n[rows, :] / acc_d[rows, :]).astype(BF)

    def ffn_input(att, tokens, row_of):
        stream = tokens + jnp.dot(att, wo[...], preferred_element_type=F32)
        place = lat * SIDE + row_of - 1
        inside = (place >= 0) & (place < n_lat * SIDE)
        return jnp.where(inside, norm_rows(stream, gf[...]), 0.0).astype(BF)

    def up_project(count, hid):
        for t in range(HID // 512):
            cols = slice(t * 512, (t + 1) * 512)
            hidden = jnp.dot(nf[:count, :], wu[:, cols], preferred_element_type=F32)
            hid[:count, cols] = hidden.astype(BF).astype(F32)

    sub = iota((8, TILE), 0)

    def filter_half(side, hid, west_row, east_row):
        @pl.loop(0, HID // TILE)
        def _(t):
            cols = pl.ds(pl.multiple_of(t * TILE, TILE), TILE)
            tap = [[taps[a, pl.ds(b, 1), cols] for b in range(3)] for a in range(3)]
            total = [None] * RING
            for g in range(RING):
                mid = hid[g * 8 : g * 8 + 8, cols]
                w_edge, e_edge = west_row(g, cols), east_row(g, cols)
                lower = jnp.where(sub == 0, w_edge, pltpu.roll(mid, 1, 0))
                upper = jnp.where(sub == 7, e_edge, pltpu.roll(mid, 7, 0))
                for a in range(3):
                    r = g - a
                    if 0 <= r < SIDE:
                        term = lower * tap[a][0] + mid * tap[a][1] + upper * tap[a][2]
                        total[r] = term if total[r] is None else total[r] + term
                if g >= 2:
                    r = g - 2
                    out[r, side * 8 : side * 8 + 8, cols] = gelu(total[r]).astype(BF)

    side_middle(et)
    arrived(W_LOW)
    start(W_DOWN)
    start(W_UP2)
    arrived(E_DOWN)
    arrived(E_UP)
    arrived(E_UP2)
    edge = side_attention(1, et)
    arrived(W_HIGH)
    start(W_UP)
    loc[L_GF].wait()
    loc[L_TAPS].wait()
    loc[L_WO].wait()
    loc[L_WU].wait()
    slot, source = iota((EDGE, HALF), 0), iota((EDGE, HALF), 1)
    pick = jnp.where((source == slot * 8 + 7) & (slot < RING), 1.0, 0.0).astype(BF)
    att = jnp.dot(pick, attended(slice(0, HALF)), preferred_element_type=F32).astype(BF)
    slot, source = iota((EDGE, KEYS_C), 0), iota((EDGE, KEYS_C), 1)
    pick = (source == (slot + REACH - 1) * SIDE + 7) & (slot < RING)
    pick = jnp.where(pick, 1.0, 0.0).astype(BF)
    tokens = jnp.dot(pick, ct[...].reshape(KEYS_C, D), preferred_element_type=F32)
    nf[...] = ffn_input(
        jnp.concatenate([attended(slice(HALF, 2 * HALF + EDGE)), att], 0),
        jnp.concatenate([xres[HALF:, :], edge, tokens], 0),
        jnp.concatenate([h >> 3, e, e], 0),
    )

    up_project(HALF + 2 * EDGE, hid_r)
    side_middle(wt)
    filter_half(
        1, hid_r,
        lambda g, cols: hid_r[HALF + EDGE + g : HALF + EDGE + g + 1, cols],
        lambda g, cols: hid_r[HALF + g : HALF + g + 1, cols],
    )

    arrived(W_DOWN)
    arrived(W_UP)
    arrived(W_UP2)
    edge = side_attention(0, wt)
    nf[: HALF + EDGE, :] = ffn_input(
        jnp.concatenate([attended(slice(0, HALF)), attended(edge_rows)], 0),
        jnp.concatenate([xres[:HALF, :], edge], 0),
        jnp.concatenate([h >> 3, e], 0),
    )
    up_project(HALF + EDGE, hid_l)
    filter_half(
        0, hid_l,
        lambda g, cols: hid_l[HALF + g : HALF + g + 1, cols],
        lambda g, cols: hid_r[g * 8 : g * 8 + 1, cols],
    )
    for i in range(len(rem)):
        sent(i)


def on_device(tokens, gain_attn, w_qkv, logit_scale, w_out, gain_ffn, w_up, conv_taps):
    vm = pltpu.VMEM
    anywhere = pl.BlockSpec(memory_space=pl.ANY)
    return pl.pallas_call(
        kernel,
        out_shape=jax.ShapeDtypeStruct((SIDE, SIDE, HID), BF),
        in_specs=[anywhere] * 8,
        out_specs=pl.BlockSpec(memory_space=pltpu.VMEM),
        scratch_shapes=[
            vm((32, SIDE, D), BF),
            vm((KEYS_S, D), BF),
            vm((KEYS_S, D), BF),
            vm((KEYS_C, D), BF),
            vm((STRIP, D), BF),
            vm((STRIP, D), BF),
            vm((D, INNER), BF),
            vm((D, INNER), BF),
            vm((D, INNER), BF),
            vm((INNER, D), BF),
            vm((D, HID), BF),
            vm((1, D), F32),
            vm((1, D), F32),
            vm((3, 3, HID), F32),
            vm((KEYS_C, INNER), BF),
            vm((PAIRS, KEYS_C, 256), BF),
            vm((KEYS_S, INNER), BF),
            vm((PAIRS, KEYS_S, 256), BF),
            vm((2 * HALF, INNER), BF),
            vm((HALF + EDGE, INNER), BF),
            vm((2 * HALF, D), F32),
            vm((2 * HALF + EDGE, INNER), F32),
            vm((2 * HALF + EDGE, INNER), F32),
            vm((2 * HALF, KEYS_C), F32),
            vm((2, HALF + EDGE, KEYS_S), F32),
            vm((2, EDGE, KEYS_C), F32),
            vm((HALF + 2 * EDGE, D), BF),
            vm((HALF + EDGE, HID), F32),
            vm((HALF + 2 * EDGE, HID), F32),
            pltpu.SMEM((HEADS,), F32),
            pltpu.SemaphoreType.DMA((10,)),
            pltpu.SemaphoreType.DMA((12,)),
            pltpu.SemaphoreType.DMA((12,)),
        ],
        compiler_params=pltpu.CompilerParams(
            collective_id=0, has_side_effects=True, vmem_limit_bytes=52 * 2**20
        ),
        name="weather_block",
    )(
        *(pltpu.with_memory_space_constraint(x, pltpu.HBM) for x in (
            tokens, gain_attn.reshape(1, D), w_qkv, logit_scale, w_out,
            gain_ffn.reshape(1, D), w_up, conv_taps,
        ))
    )


def solution(mesh):
    in_specs = (P("lat", "lon", None), P(), P(), P(), P(), P(), P(), P())
    return jax.shard_map(
        on_device, mesh=mesh, in_specs=in_specs, out_specs=P("lat", "lon", None), check_vma=False
    )
```

```python
import functools

import jax
import jax.numpy as jnp
from jax import lax
from jax.experimental import pallas as pl
from jax.experimental.pallas import tpu as pltpu
from jax.sharding import PartitionSpec as P

D = 1024
HEADS = 8
HEAD_DIM = 64
HID = 2048
RADIUS = 6
INNER = 512

SIDE = 16
REACH = RADIUS + 1
ROWS = SIDE + 2 * REACH
RING = SIDE + 2
HALF = RING * 8
EDGE = 32
STRIP = SIDE * REACH
CORNER = 64
CUT = STRIP - CORNER
KEYS_C = 512
KEYS_S = 256
PAIRS = HEADS // 2
TILE = 256
BF = jnp.bfloat16
F32 = jnp.float32
MESH = pl.DeviceIdType.MESH
FAR = -1e30

DOWN, UP, W_LOW, W_HIGH, E_LOW, E_HIGH, W_DOWN, W_UP, E_DOWN, E_UP, W_UP2, E_UP2 = range(12)
L_TOK, L_GA, L_GF, L_TAPS, L_WK, L_WV, L_WQ, L_WO, L_WU, L_SCALE = range(10)


def iota(shape, dim):
    return lax.broadcasted_iota(jnp.int32, shape, dim)


def div7(n):
    return (n * 9363) >> 16


def norm_rows(x, gain):
    centre = jnp.mean(x, -1, keepdims=True)
    moved = x - centre
    spread = jnp.mean(moved * moved, -1, keepdims=True)
    return moved * lax.rsqrt(spread + 1e-05) * gain


def gelu(x):
    size = jnp.abs(x)
    t = 1.0 / (1.0 + size * (0.3275911 * 0.7071067811865476))
    poly = 0.5 * 1.061405429
    for c in (-1.453152027, 1.421413741, -0.284496736, 0.254829592):
        poly = poly * t + 0.5 * c
    tail = poly * t * jnp.exp(x * x * -0.5)
    return jnp.maximum(x, 0.0) - size * tail


def kernel(
    tok, ga_h, wqkv_h, scale_h, wo_h, gf_h, wu_h, taps_h, out,
    ct, wt, et, xn, send_e, send_w, wk, wv, wq, wo, wu, ga, gf, taps,
    kc, vc, kw, vw, qc, qe, xres, acc_n, acc_d, bias_c, bias_s, bias_e,
    nf, hid_l, hid_r, scale, lsem, ss, rs,
):
    lat, lon = lax.axis_index("lat"), lax.axis_index("lon")
    n_lat, n_lon = lax.axis_size("lat"), lax.axis_size("lon")
    east, west = lax.rem(lon + 1, n_lon), lax.rem(lon + n_lon - 1, n_lon)
    north_ok, south_ok = lat > 0, lat < n_lat - 1

    loc = [
        pltpu.make_async_copy(s, d, lsem.at[i])
        for i, (s, d) in enumerate((
            (tok, ct.at[pl.ds(REACH, SIDE)]),
            (ga_h, ga), (gf_h, gf), (taps_h, taps),
            (wqkv_h.at[:, pl.ds(INNER, INNER)], wk),
            (wqkv_h.at[:, pl.ds(2 * INNER, INNER)], wv),
            (wqkv_h.at[:, pl.ds(0, INNER)], wq),
            (wo_h, wo), (wu_h, wu), (scale_h, scale),
        ))
    ]
    loc[L_TOK].start()

    def remote(i, src, dst, device):
        return pltpu.make_async_remote_copy(
            src_ref=src, dst_ref=dst, send_sem=ss.at[i], recv_sem=rs.at[i],
            device_id=device, device_id_type=MESH,
        )

    below, above = (lat + 1, lon), (lat - 1, lon)
    to_e, to_w = (lat, east), (lat, west)
    low, high = pl.ds(CUT, CORNER), pl.ds(0, CUT)
    low_d, high_d = pl.ds(CORNER + CUT, CORNER), pl.ds(CORNER, CUT)
    top_d = pl.ds(0, CORNER)
    first_d, second_d = pl.ds(CORNER, CUT), pl.ds(CORNER + CUT, CORNER - CUT)
    bot_first = pl.ds(CORNER + STRIP, CUT)
    bot_second = pl.ds(CORNER + STRIP + CUT, CORNER - CUT)
    rem = [
        remote(DOWN, tok.at[pl.ds(SIDE - REACH, REACH)], ct.at[pl.ds(0, REACH)], below),
        remote(UP, tok.at[pl.ds(0, REACH)], ct.at[pl.ds(REACH + SIDE, REACH)], above),
        remote(W_LOW, send_e.at[low], wt.at[low_d], to_e),
        remote(W_HIGH, send_e.at[high], wt.at[high_d], to_e),
        remote(E_LOW, send_w.at[low], et.at[low_d], to_w),
        remote(E_HIGH, send_w.at[high], et.at[high_d], to_w),
        remote(W_DOWN, wt.at[low_d], wt.at[top_d], below),
        remote(W_UP, wt.at[first_d], wt.at[bot_first], above),
        remote(E_DOWN, et.at[low_d], et.at[top_d], below),
        remote(E_UP, et.at[first_d], et.at[bot_first], above),
        remote(W_UP2, wt.at[second_d], wt.at[bot_second], above),
        remote(E_UP2, et.at[second_d], et.at[bot_second], above),
    ]
    seam_top, seam_bottom = lat == n_lat // 2 - 1, lat == n_lat // 2
    seam = seam_top | seam_bottom
    head, neck = pl.ds(0, CUT), pl.ds(CUT, CORNER - CUT)
    direct_south = [
        remote(W_DOWN, send_e.at[low], wt.at[top_d], (lat + 1, east)),
        remote(E_DOWN, send_w.at[low], et.at[top_d], (lat + 1, west)),
    ]
    direct_north = [
        remote(W_UP, send_e.at[head], wt.at[bot_first], (lat - 1, east)),
        remote(E_UP, send_w.at[head], et.at[bot_first], (lat - 1, west)),
        remote(W_UP2, send_e.at[neck], wt.at[bot_second], (lat - 1, east)),
        remote(E_UP2, send_w.at[neck], et.at[bot_second], (lat - 1, west)),
    ]
    goes_south, goes_north = (DOWN, W_DOWN, E_DOWN), (UP, W_UP, E_UP, W_UP2, E_UP2)

    def start(i):
        if i in (W_DOWN, E_DOWN):
            pl.when(south_ok & jnp.logical_not(seam_top))(rem[i].start)
        elif i in (W_UP, E_UP, W_UP2, E_UP2):
            pl.when(north_ok & jnp.logical_not(seam_bottom))(rem[i].start)
        elif i in goes_south:
            pl.when(south_ok)(rem[i].start)
        elif i in goes_north:
            pl.when(north_ok)(rem[i].start)
        else:
            rem[i].start()

    def arrived(i):
        if i in goes_south:
            pl.when(north_ok)(rem[i].wait_recv)
        elif i in goes_north:
            pl.when(south_ok)(rem[i].wait_recv)
        else:
            rem[i].wait_recv()

    def sent(i):
        if i in goes_south:
            pl.when(south_ok)(rem[i].wait_send)
        elif i in goes_north:
            pl.when(north_ok)(rem[i].wait_send)
        else:
            rem[i].wait_send()

    barrier = pltpu.get_barrier_semaphore()
    for device in (to_e, to_w):
        pl.semaphore_signal(barrier, inc=1, device_id=device, device_id_type=MESH)

    for there, row in ((seam_top, lat + 1), (seam_bottom, lat - 1)):

        @pl.when(there)
        def _():
            for device in ((row, east), (row, west)):
                pl.semaphore_signal(barrier, inc=1, device_id=device, device_id_type=MESH)

    @pl.when(south_ok)
    def _():
        pl.semaphore_signal(barrier, inc=1, device_id=below, device_id_type=MESH)

    @pl.when(north_ok)
    def _():
        pl.semaphore_signal(barrier, inc=1, device_id=above, device_id_type=MESH)

    loc[L_TOK].wait()
    for c in loc[1:]:
        c.start()
    mine = ct[REACH : REACH + SIDE].reshape(SIDE * SIDE, D)
    slot, source = iota((STRIP, SIDE * SIDE), 0), iota((STRIP, SIDE * SIDE), 1)
    origin = div7(slot) * (SIDE - REACH) + slot

    def pack(offset):
        pick = jnp.where(source == origin + offset, 1.0, 0.0).astype(BF)
        return jnp.dot(pick, mine, preferred_element_type=F32).astype(BF)

    send_e[...] = pack(SIDE - REACH)
    send_w[...] = pack(0)

    @pl.when(seam)
    def _():
        pl.semaphore_wait(barrier, 6)

    @pl.when(south_ok & north_ok & jnp.logical_not(seam))
    def _():
        pl.semaphore_wait(barrier, 4)

    @pl.when(jnp.logical_not(south_ok & north_ok))
    def _():
        pl.semaphore_wait(barrier, 3)

    start(DOWN)
    start(UP)
    late = lon == n_lon - 1

    @pl.when(late)
    def _():
        for i in (W_LOW, W_HIGH, E_LOW, E_HIGH):
            start(i)

    @pl.when(jnp.logical_not(late))
    def _():
        for i in (E_LOW, E_HIGH, W_LOW, W_HIGH):
            start(i)

    def follow(i):
        pl.when(jnp.logical_not(late))(lambda: start(i))

    for there, copies in ((seam_top, direct_south), (seam_bottom, direct_north)):

        @pl.when(there)
        def _():
            for copy in copies:
                copy.start()

    ct[ROWS:, :, :] = jnp.zeros((32 - ROWS, SIDE, D), BF)
    for strip in (wt, et):
        strip[2 * CORNER + STRIP :, :] = jnp.zeros((KEYS_S - 2 * CORNER - STRIP, D), BF)

    @pl.when(lat == 0)
    def _():
        ct[:REACH, :, :] = jnp.zeros((REACH, SIDE, D), BF)
        for strip in (wt, et):
            strip[:CORNER, :] = jnp.zeros((CORNER, D), BF)

    @pl.when(lat == n_lat - 1)
    def _():
        ct[REACH + SIDE : ROWS, :, :] = jnp.zeros((REACH, SIDE, D), BF)
        for strip in (wt, et):
            strip[CORNER + STRIP : 2 * CORNER + STRIP, :] = jnp.zeros((CORNER, D), BF)

    def bias(q_row, q_col, k_row, k_col):
        place = lat * SIDE + k_row
        k_row = jnp.where((place >= 0) & (place < n_lat * SIDE), k_row, 1000)
        near = (jnp.abs(k_row - q_row) <= RADIUS) & (jnp.abs(k_col - q_col) <= RADIUS)
        return jnp.where(near, 0.0, FAR)

    m = iota((2 * HALF, 1), 0)
    right = jnp.where(m >= HALF, 1, 0)
    qc_row = ((m - right * HALF) >> 3) - 1
    qc_col = (m & 7) + 8 * right
    n = iota((1, KEYS_C), 1)
    kc_row = jnp.where(n < ROWS * SIDE, (n >> 4) - REACH, 1000)
    kc_col = n & 15
    bias_c[...] = bias(qc_row, qc_col, kc_row, kc_col)
    j = iota((1, KEYS_S), 1)
    ks_row7 = div7(j + 6)
    ks_row = jnp.where(j < 2 * CORNER + STRIP, ks_row7 - 10, 1000)
    ks_col = j + 6 - 7 * ks_row7
    e = iota((EDGE, 1), 0)
    h = iota((HALF, 1), 0)
    main_row, main_col = (h >> 3) - 1, h & 7
    for side, (first_q, edge_q, first_k) in enumerate(((0, -1, -REACH), (8, SIDE, SIDE))):
        bias_s[side, :HALF, :] = bias(main_row, main_col + first_q, ks_row, ks_col + first_k)
        bias_s[side, HALF:, :] = bias(e - 1, edge_q, ks_row, ks_col + first_k)
        bias_e[side] = bias(e - 1, edge_q, kc_row, kc_col)

    loc[L_SCALE].wait()
    lane = iota((1, INNER), 1)
    factor = jnp.zeros((1, INNER), F32)
    for head in range(HEADS):
        factor = jnp.where((lane >> 6) == head, scale[head], factor)
    block = jnp.where(
        (iota((TILE, TILE), 0) >> 6) == (iota((TILE, TILE), 1) >> 6), 1.0, 0.0
    ).astype(BF)
    first_head = (iota((1, 128), 1) < HEAD_DIM)

    for vv in (vc, vw):
        vv[:, :, 128:] = jnp.ones((PAIRS, vv.shape[1], 128), BF)

    def unit(x):
        square = x * x
        top = square.astype(BF)
        rest = (square - top.astype(F32)).astype(BF)
        totals = []
        for t in range(INNER // TILE):
            cols = slice(t * TILE, (t + 1) * TILE)
            totals.append(
                jnp.dot(top[:, cols], block, preferred_element_type=F32)
                + jnp.dot(rest[:, cols], block, preferred_element_type=F32)
            )
        return x * lax.rsqrt(jnp.concatenate(totals, 1) + 1e-06)

    def keys_values(x, pieces, k_dst, v_dst):
        keys = jnp.dot(x, wk[...], preferred_element_type=F32)
        values = jnp.dot(x, wv[...], preferred_element_type=F32).astype(BF)
        keys = unit(keys).astype(BF)
        for first, start_row, count in pieces:
            k_dst[start_row : start_row + count, :] = keys[first : first + count]
            for p in range(PAIRS):
                v_dst[p, start_row : start_row + count, :128] = values[
                    first : first + count, 128 * p : 128 * p + 128
                ]

    def attend(q, k_src, v_src, bias_ref, take):
        count = q.shape[0]
        scores = []
        for p in range(PAIRS):
            qp = q[:, 128 * p : 128 * p + 128]
            zero = jnp.zeros_like(qp)
            both = jnp.concatenate(
                [jnp.where(first_head, qp, zero), jnp.where(first_head, zero, qp)], 0
            )
            scores.append(lax.dot_general(
                both, k_src[:, 128 * p : 128 * p + 128], (((1,), (1,)), ((), ())),
                preferred_element_type=F32,
            ))
        term = bias_ref[...]
        for p in range(PAIRS):
            weights = jnp.concatenate(
                [
                    jnp.exp(scores[p][:count] + term).astype(BF),
                    jnp.exp(scores[p][count:] + term).astype(BF),
                ],
                0,
            )
            summed = jnp.dot(weights, v_src[p], preferred_element_type=F32)
            take(
                slice(128 * p, 128 * p + 128),
                jnp.where(first_head, summed[:count, :128], summed[count:, :128]),
                jnp.where(first_head, summed[:count, 128:], summed[count:, 128:]),
            )

    loc[L_GA].wait()
    gain = ga[...]
    own = REACH * SIDE
    xn[own : own + SIDE * SIDE, :] = norm_rows(mine.astype(F32), gain).astype(BF)
    loc[L_WK].wait()
    loc[L_WV].wait()
    keys_values(xn[own : own + SIDE * SIDE, :], ((0, own, SIDE * SIDE),), kc, vc)

    arrived(DOWN)
    arrived(UP)
    tail_rows = (32 - REACH - SIDE) * SIDE
    tail = own + SIDE * SIDE
    x = jnp.concatenate(
        [
            ct[:REACH].reshape(own, D).astype(F32),
            ct[REACH + SIDE :].reshape(tail_rows, D).astype(F32),
        ],
        0,
    )
    x = norm_rows(x, gain).astype(BF)
    xn[:own, :] = x[:own]
    xn[tail:, :] = x[own:]
    keys_values(x, ((0, 0, own), (own, tail, tail_rows)), kc, vc)
    arrived(E_LOW)
    start(E_DOWN)
    start(E_UP2)

    def halves(x):
        x = x.reshape(RING, 2, 8, x.shape[-1])
        return [x[:, s].reshape(HALF, x.shape[-1]) for s in range(2)]

    ring = pl.ds((REACH - 1) * SIDE, RING * SIDE)
    for s, part in enumerate(halves(ct[REACH - 1 : REACH + SIDE + 1].reshape(RING * SIDE, D).astype(F32))):
        xres[s * HALF : (s + 1) * HALF, :] = part
    loc[L_WQ].wait()
    q = unit(jnp.dot(xn[ring, :], wq[...], preferred_element_type=F32)) * factor
    for s, part in enumerate(halves(q)):
        qc[s * HALF : (s + 1) * HALF, :] = part.astype(BF)

    def keep(cols, num, den):
        acc_n[: 2 * HALF, cols] = num
        acc_d[: 2 * HALF, cols] = den

    arrived(E_HIGH)
    start(E_UP)
    attend(qc[...], kc, vc, bias_c, keep)

    edge_rows = slice(2 * HALF, 2 * HALF + EDGE)
    strip_end = CORNER + STRIP

    def side_middle(strip):
        x = norm_rows(strip[CORNER:strip_end, :].astype(F32), gain).astype(BF)
        keys_values(x, ((0, CORNER, STRIP),), kw, vw)

    def side_attention(side, strip):
        last = KEYS_S - strip_end
        slot, source = iota((EDGE, KEYS_S), 0), iota((EDGE, KEYS_S), 1)
        first = (CORNER + REACH - 1, CORNER)[side] - REACH
        pick = jnp.where((source == slot * REACH + first) & (slot < RING), 1.0, 0.0).astype(BF)
        edge = jnp.dot(pick, strip[...], preferred_element_type=F32)
        x = jnp.concatenate([strip[:CORNER, :], strip[strip_end:, :]], 0).astype(F32)
        x = norm_rows(x, gain).astype(BF)
        keys_values(x, ((0, 0, CORNER), (CORNER, strip_end, last)), kw, vw)
        xe = norm_rows(edge, gain).astype(BF)
        q = unit(jnp.dot(xe, wq[...], preferred_element_type=F32)) * factor
        qe[HALF:, :] = q.astype(BF)
        main = slice(side * HALF, side * HALF + HALF)
        qe[:HALF, :] = qc[main, :]

        def first_edge(cols, num, den):
            acc_n[edge_rows, cols] = num
            acc_d[edge_rows, cols] = den

        attend(qe[HALF:, :], kc, vc, bias_e.at[side], first_edge)

        def add(cols, num, den):
            acc_n[main, cols] += num[:HALF]
            acc_d[main, cols] += den[:HALF]
            acc_n[edge_rows, cols] += num[HALF:]
            acc_d[edge_rows, cols] += den[HALF:]

        attend(qe[...], kw, vw, bias_s.at[side], add)
        return edge

    def attended(rows):
        return (acc_n[rows, :] / acc_d[rows, :]).astype(BF)

    def ffn_input(att, tokens, row_of):
        stream = tokens + jnp.dot(att, wo[...], preferred_element_type=F32)
        place = lat * SIDE + row_of - 1
        inside = (place >= 0) & (place < n_lat * SIDE)
        return jnp.where(inside, norm_rows(stream, gf[...]), 0.0).astype(BF)

    def up_project(count, hid):
        for t in range(HID // 512):
            cols = slice(t * 512, (t + 1) * 512)
            hidden = jnp.dot(nf[:count, :], wu[:, cols], preferred_element_type=F32)
            hid[:count, cols] = hidden.astype(BF).astype(F32)

    sub = iota((8, TILE), 0)

    def filter_half(side, hid, west_row, east_row):
        @pl.loop(0, HID // TILE)
        def _(t):
            cols = pl.ds(pl.multiple_of(t * TILE, TILE), TILE)
            tap = [[taps[a, pl.ds(b, 1), cols] for b in range(3)] for a in range(3)]
            total = [None] * RING
            for g in range(RING):
                mid = hid[g * 8 : g * 8 + 8, cols]
                w_edge, e_edge = west_row(g, cols), east_row(g, cols)
                lower = jnp.where(sub == 0, w_edge, pltpu.roll(mid, 1, 0))
                upper = jnp.where(sub == 7, e_edge, pltpu.roll(mid, 7, 0))
                for a in range(3):
                    r = g - a
                    if 0 <= r < SIDE:
                        term = lower * tap[a][0] + mid * tap[a][1] + upper * tap[a][2]
                        total[r] = term if total[r] is None else total[r] + term
                if g >= 2:
                    r = g - 2
                    out[r, side * 8 : side * 8 + 8, cols] = gelu(total[r]).astype(BF)

    side_middle(et)
    arrived(W_LOW)
    start(W_DOWN)
    start(W_UP2)
    arrived(E_DOWN)
    arrived(E_UP)
    arrived(E_UP2)
    arrived(W_HIGH)
    start(W_UP)
    edge = side_attention(1, et)
    loc[L_GF].wait()
    loc[L_TAPS].wait()
    loc[L_WO].wait()
    loc[L_WU].wait()
    slot, source = iota((EDGE, HALF), 0), iota((EDGE, HALF), 1)
    pick = jnp.where((source == slot * 8 + 7) & (slot < RING), 1.0, 0.0).astype(BF)
    att = jnp.dot(pick, attended(slice(0, HALF)), preferred_element_type=F32).astype(BF)
    slot, source = iota((EDGE, KEYS_C), 0), iota((EDGE, KEYS_C), 1)
    pick = (source == (slot + REACH - 1) * SIDE + 7) & (slot < RING)
    pick = jnp.where(pick, 1.0, 0.0).astype(BF)
    tokens = jnp.dot(pick, ct[...].reshape(KEYS_C, D), preferred_element_type=F32)
    nf[...] = ffn_input(
        jnp.concatenate([attended(slice(HALF, 2 * HALF + EDGE)), att], 0),
        jnp.concatenate([xres[HALF:, :], edge, tokens], 0),
        jnp.concatenate([h >> 3, e, e], 0),
    )

    up_project(HALF + 2 * EDGE, hid_r)
    side_middle(wt)
    filter_half(
        1, hid_r,
        lambda g, cols: hid_r[HALF + EDGE + g : HALF + EDGE + g + 1, cols],
        lambda g, cols: hid_r[HALF + g : HALF + g + 1, cols],
    )

    arrived(W_DOWN)
    arrived(W_UP)
    arrived(W_UP2)
    edge = side_attention(0, wt)
    nf[: HALF + EDGE, :] = ffn_input(
        jnp.concatenate([attended(slice(0, HALF)), attended(edge_rows)], 0),
        jnp.concatenate([xres[:HALF, :], edge], 0),
        jnp.concatenate([h >> 3, e], 0),
    )
    up_project(HALF + EDGE, hid_l)
    filter_half(
        0, hid_l,
        lambda g, cols: hid_l[HALF + g : HALF + g + 1, cols],
        lambda g, cols: hid_r[g * 8 : g * 8 + 1, cols],
    )
    for i in range(len(rem)):
        sent(i)


def on_device(tokens, gain_attn, w_qkv, logit_scale, w_out, gain_ffn, w_up, conv_taps):
    vm = pltpu.VMEM
    anywhere = pl.BlockSpec(memory_space=pl.ANY)
    return pl.pallas_call(
        kernel,
        out_shape=jax.ShapeDtypeStruct((SIDE, SIDE, HID), BF),
        in_specs=[anywhere] * 8,
        out_specs=pl.BlockSpec(memory_space=pltpu.VMEM),
        scratch_shapes=[
            vm((32, SIDE, D), BF),
            vm((KEYS_S, D), BF),
            vm((KEYS_S, D), BF),
            vm((KEYS_C, D), BF),
            vm((STRIP, D), BF),
            vm((STRIP, D), BF),
            vm((D, INNER), BF),
            vm((D, INNER), BF),
            vm((D, INNER), BF),
            vm((INNER, D), BF),
            vm((D, HID), BF),
            vm((1, D), F32),
            vm((1, D), F32),
            vm((3, 3, HID), F32),
            vm((KEYS_C, INNER), BF),
            vm((PAIRS, KEYS_C, 256), BF),
            vm((KEYS_S, INNER), BF),
            vm((PAIRS, KEYS_S, 256), BF),
            vm((2 * HALF, INNER), BF),
            vm((HALF + EDGE, INNER), BF),
            vm((2 * HALF, D), F32),
            vm((2 * HALF + EDGE, INNER), F32),
            vm((2 * HALF + EDGE, INNER), F32),
            vm((2 * HALF, KEYS_C), F32),
            vm((2, HALF + EDGE, KEYS_S), F32),
            vm((2, EDGE, KEYS_C), F32),
            vm((HALF + 2 * EDGE, D), BF),
            vm((HALF + EDGE, HID), F32),
            vm((HALF + 2 * EDGE, HID), F32),
            pltpu.SMEM((HEADS,), F32),
            pltpu.SemaphoreType.DMA((10,)),
            pltpu.SemaphoreType.DMA((12,)),
            pltpu.SemaphoreType.DMA((12,)),
        ],
        compiler_params=pltpu.CompilerParams(
            collective_id=0, has_side_effects=True, vmem_limit_bytes=52 * 2**20
        ),
        name="weather_block",
    )(
        *(pltpu.with_memory_space_constraint(x, pltpu.HBM) for x in (
            tokens, gain_attn.reshape(1, D), w_qkv, logit_scale, w_out,
            gain_ffn.reshape(1, D), w_up, conv_taps,
        ))
    )


def solution(mesh):
    in_specs = (P("lat", "lon", None), P(), P(), P(), P(), P(), P(), P())
    return jax.shard_map(
        on_device, mesh=mesh, in_specs=in_specs, out_specs=P("lat", "lon", None), check_vma=False
    )
```
